256 devices in a mesh: dp: 8 (over x, core), expert: 32 (over y, z).
Axes of the slice: x: 4, y: 4, z: 8, core: 2. Of those that a mesh axis runs over, the one named last changes fastest.
Arguments:
- out_grad: bfloat16 [49152, 4096], P(('dp', 'expert')), may hold values from -24 to 24
- route_gates: float32 [49152, 8], P(('dp', 'expert')), may hold values from 0.02 to 0.4
- expert_ids: int32 [49152, 8], P(('dp', 'expert')), may hold values from 0 to 127, all different within a row; in each aligned block of 192 rows (0 to 191, 192 to 383, ...) at most 18 rows name the same one
- partner_offset: int32 [32], P('expert'), may hold values from 1 to 7
- saved_pre: bfloat16 [8, 32, 576, 1536], P('dp', 'expert'), may hold values from -6 to 6
- down_weight: bfloat16 [32, 768, 4096], P('expert', None, 'dp'), may hold values from -0.21875 to 0.21875
- gate_up_weight: bfloat16 [32, 4096, 1536], P('expert', 'dp'), may hold values from -0.09375 to 0.09375
Outputs:
- token_grad: bfloat16 [49152, 4096], P(('dp', 'expert'))
- hidden_grad: bfloat16 [8, 32, 576, 1536], P('dp', 'expert')
The draws below stay inside these ranges and needn't reach their ends.
Inputs may be any that keep to these rules, and one draw needn't show every extreme that they name: `expert_ids`: each row names 8 different experts; among the rows of one device no expert is named by more than 18 rows.
All inputs are finite; a program needn't handle non-finite values.
Results may differ from the reference program's by a relative error of at most 0.0064.
Values may be sent and summed in bfloat16 or wider, within the bound.
No kernel may reach another device: no remote copies, remote signals or barrier semaphores. Data moves between devices by JAX's collectives and lax.ppermute only.
A program may use at most 128 MiB of HBM per device.

```python
import math
import jax
import jax.numpy as jnp
import numpy as np
from jax import lax

D = 4096
ALL_EXP = 128
TOPK = 8
H = 768
TOK_DEV = 192
CAP = 15
OC = 3
MOST = 18
EXPERTS = 32
TOKENS = 49152
SLOTS = 576
N_DP = 8
N_EXPERT = 32


def plant(values, own_key, smallest, high):
    extent = values.shape
    spot = [jax.random.randint(jax.random.fold_in(own_key, axis), (), 0, extent[axis]) for axis in range(len(extent))]
    values = values.at[tuple(spot)].set(smallest)
    longest = extent.index(max(extent))
    spot[longest] = (spot[longest] + 1) % extent[longest]
    return values.at[tuple(spot)].set(high)


def steps_of(own_key, dims, cuts, low, high):
    def one(dim, blocks):
        heights = jax.random.uniform(jax.random.fold_in(jax.random.fold_in(own_key, 6), dim), (blocks,), jnp.float32, low / len(cuts), high / len(cuts))
        return jnp.repeat(jnp.exp(heights), dims[dim] // blocks).reshape((-1,) + (1,) * (len(dims) - dim - 1))

    factor_of = one(*cuts[0])
    for cut in cuts[1:]:
        factor_of = factor_of * one(*cut)
    return factor_of


def assign_block(key, own, number, rows, count, top, reach, skew):
    ranking = jax.random.permutation(key, count)
    heavy_load, usual = load_shares(count, rows * top, reach, skew, True), load_shares(count, rows * top, reach, skew, False)
    places = jnp.arange(count)

    def named(tallies, rotation):
        used = int((tallies > 0).sum())
        fixed = max(1, used // 4)
        passed = fixed + (places - fixed + rotation * (used - fixed)) % max(1, count - fixed)
        return jnp.zeros((count,), jnp.int32).at[ranking[jnp.where(places < fixed, places, passed)]].set(jnp.asarray(tallies, jnp.int32))

    tallies = jnp.where(number % 4 == 0, named(heavy_load, number // 4), named(usual, number - number // 4 - 1))
    mixed = jax.random.permutation(jax.random.fold_in(own, 3), count)
    giver, sink = mixed[0:count // 2 * 2:2], mixed[1:count // 2 * 2:2]
    room = jnp.minimum(tallies[giver] - 1, reach - tallies[sink]) // 2
    room = jnp.where((giver == ranking[0]) | (sink == ranking[0]) | (tallies[sink] == 0), 0, jnp.maximum(room, 0))
    passed = jax.random.randint(jax.random.fold_in(own, 4), (count // 2,), 0, 1 << 20) % (room + 1)
    tallies = tallies.at[giver].add(-passed).at[sink].add(passed)
    items = jnp.searchsorted(jnp.cumsum(tallies), jnp.arange(rows * top), side="right").astype(jnp.int32)
    listing = items.reshape(top, rows).T
    listing = listing[jax.random.permutation(jax.random.fold_in(own, 1), rows)]
    rotation = jax.random.randint(jax.random.fold_in(own, 2), (rows, 1), 0, top)
    return jnp.take_along_axis(listing, (jnp.arange(top)[None, :] + rotation) % top, axis=1)


def load_shares(number_of, total, bound, skew, full):
    portions = [(1 << 20) // math.isqrt(standing ** skew) + 1 for standing in range(1, number_of + 1)]
    largest = bound if full else min(bound, max(-(-total // number_of), total * portions[0] // sum(portions)))
    least = 1 if total - largest >= number_of - 1 else 0
    holding, rest = [largest] + [least] * (number_of - 1), total - largest - least * (number_of - 1)
    while rest > 0:
        free = [i for i in range(1, number_of) if holding[i] < largest] or [i for i in range(1, number_of) if holding[i] < bound]
        whole, left = sum([portions[i] for i in free]), rest
        for i in free:
            addition = min(bound - holding[i], max(1, left * portions[i] // whole), rest)
            holding[i] = holding[i] + addition
            rest = rest - addition
    return np.array(holding)


def noise(own_key, shape, spread, bound, cuts=(), held_as=jnp.bfloat16):
    result = spread * jax.random.normal(own_key, shape, jnp.float32)
    if cuts:
        result = result * steps_of(own_key, shape, cuts, -0.22, 0.18)
    return jnp.clip(result, -bound, bound).astype(held_as)


def setup_inputs(seed: int = 0) -> dict:
    splits = jax.random.split(jax.random.key(seed), 8)
    out_grad = noise(splits[0], (TOKENS, D), 4.0, 24.0, ((0, 256),))
    route_gates = jnp.clip(jnp.exp(math.log(0.4) - 2.9957323 * jax.random.uniform(splits[1], (TOKENS, TOPK), jnp.float32) ** steps_of(splits[1], (TOKENS, TOPK), ((0, 256),), -0.2, 0.2)), 0.02, 0.4)
    expert_ids_keys = jax.random.split(jax.random.fold_in(splits[2], 1), TOKENS // TOK_DEV)
    expert_ids_turns = jax.random.permutation(jax.random.fold_in(splits[2], 3), TOKENS // TOK_DEV)
    expert_ids = jax.vmap(lambda own, number: assign_block(jax.random.fold_in(splits[2], 2), own, number, TOK_DEV, ALL_EXP, TOPK, MOST, 1))(expert_ids_keys, expert_ids_turns).reshape((TOKENS, TOPK))
    partner_offset = plant(jax.random.randint(splits[3], (EXPERTS,), 1, N_DP), jax.random.fold_in(splits[3], 1), 1, N_DP - 1).astype(jnp.int32)
    saved_pre = noise(splits[4], (N_DP, EXPERTS, SLOTS, 2 * H), 1.5, 6.0, ((0, 8), (1, 32)))
    down_weight = noise(splits[5], (EXPERTS, H, D), H ** -0.5, 0.21875, ((0, 32), (2, 8)))
    gate_up_weight = noise(splits[6], (EXPERTS, D, 2 * H), D ** -0.5, 0.09375, ((0, 32), (1, 8)))
    return {"out_grad": out_grad, "route_gates": route_gates, "expert_ids": expert_ids, "partner_offset": partner_offset, "saved_pre": saved_pre, "down_weight": down_weight, "gate_up_weight": gate_up_weight}


def route_ranks(route_ids):
    onehot = (route_ids[:, None] == jnp.arange(ALL_EXP, dtype=jnp.int32)[None, :]).astype(jnp.int32)
    before = jnp.cumsum(onehot, axis=0) - onehot
    return jnp.sum(before * onehot, axis=1).astype(jnp.int32)


def reference(out_grad, route_gates, expert_ids, partner_offset, saved_pre, down_weight, gate_up_weight):
    devices = N_DP * N_EXPERT
    ids_dev = expert_ids.reshape(devices, TOK_DEV * TOPK)
    slot_rank = jax.vmap(route_ranks)(ids_dev)
    device_index = jnp.arange(devices, dtype=jnp.int32)[:, None]
    home_replica = device_index // N_EXPERT
    source_shard = device_index % N_EXPERT
    in_window = ids_dev < EXPERTS
    in_place = slot_rank < CAP
    safe_expert = jnp.clip(ids_dev, 0, EXPERTS - 1).astype(jnp.int32)
    shift_amount = partner_offset[safe_expert]
    target_replica = jnp.where(in_place, home_replica, (home_replica + shift_amount) % N_DP).astype(jnp.int32)
    slot_row = jnp.where(in_place, source_shard * CAP + slot_rank,
                         N_EXPERT * CAP + source_shard * OC + slot_rank - CAP).astype(jnp.int32)
    flat_place = (target_replica * EXPERTS + safe_expert) * SLOTS + slot_row
    flat_place = jnp.where(in_window, flat_place, N_DP * EXPERTS * SLOTS).astype(jnp.int32)
    route_index = jnp.arange(devices * TOK_DEV * TOPK, dtype=jnp.int32)
    route_table = jnp.full((N_DP * EXPERTS * SLOTS,), -1, jnp.int32)
    route_table = route_table.at[flat_place.reshape(-1)].set(route_index, mode="drop")
    route_table = route_table.reshape(N_DP, EXPERTS, SLOTS)
    flat_gates = route_gates.reshape(-1)

    def one_expert(expert_index):
        table_rows = lax.dynamic_index_in_dim(route_table, expert_index, 1, keepdims=False).reshape(-1)
        filled = table_rows >= 0
        safe_index = jnp.where(filled, table_rows, 0).astype(jnp.int32)
        token_index = (safe_index // TOPK).astype(jnp.int32)
        gate_value = jnp.where(filled, flat_gates[safe_index], 0.0)
        cotangent = (gate_value[:, None] * out_grad[token_index].astype(jnp.float32)).astype(jnp.bfloat16)
        down_one = lax.dynamic_index_in_dim(down_weight, expert_index, 0, keepdims=False)
        hidden_cot = jnp.dot(cotangent, down_one.T, preferred_element_type=jnp.float32)
        pre_acts = lax.dynamic_index_in_dim(saved_pre, expert_index, 1, keepdims=False)
        pre_acts = pre_acts.reshape(N_DP * SLOTS, 2 * H).astype(jnp.float32)
        gate_pre = pre_acts[:, :H]
        up_pre = pre_acts[:, H:]
        sigma_gate = jax.nn.sigmoid(gate_pre)
        hidden_grad = jnp.concatenate(
            [hidden_cot * up_pre * sigma_gate * (1.0 + gate_pre * (1.0 - sigma_gate)),
             hidden_cot * gate_pre * sigma_gate], axis=1).astype(jnp.bfloat16)
        gate_up_one = lax.dynamic_index_in_dim(gate_up_weight, expert_index, 0, keepdims=False)
        row_grad = jnp.dot(hidden_grad, gate_up_one.T, preferred_element_type=jnp.float32).astype(jnp.bfloat16)
        return hidden_grad.reshape(N_DP, SLOTS, 2 * H), row_grad.reshape(N_DP, SLOTS, D)

    hidden_all, rows_all = lax.map(one_expert, jnp.arange(EXPERTS, dtype=jnp.int32))
    hidden_out = jnp.transpose(hidden_all, (1, 0, 2, 3))
    position = (safe_expert * N_DP + target_replica) * SLOTS + slot_row
    position = jnp.where(in_window, position, 0).astype(jnp.int32)
    flat_rows = rows_all.reshape(-1, D)

    def block_sum(blocks):
        positions, live_block = blocks
        picked = flat_rows[positions].astype(jnp.float32)
        return jnp.sum(jnp.where(live_block[:, :, None], picked, 0.0), axis=1).astype(jnp.bfloat16)

    token_grad = lax.map(block_sum, (position.reshape(devices, TOK_DEV, TOPK),
                                     in_window.reshape(devices, TOK_DEV, TOPK)))
    return token_grad.reshape(TOKENS, D), hidden_out
```

```python
import functools

import jax
import jax.numpy as jnp
from jax import lax
from jax.experimental import pallas as pl
from jax.experimental.pallas import tpu as pltpu
from jax.sharding import PartitionSpec as P

CAP = 15
OC = 3
MAIN = 16
CUTS = 8
F32 = jnp.float32
BF16 = jnp.bfloat16


def iota(shape, axis):
    return lax.broadcasted_iota(jnp.int32, shape, axis)


def rows_dot(left, right):
    return lax.dot_general(left, right, (((1,), (1,)), ((), ())), preferred_element_type=F32)


def plain_dot(left, right):
    return lax.dot_general(left, right, (((1,), (0,)), ((), ())), preferred_element_type=F32)


def whole(shape):
    return pl.BlockSpec(shape, lambda step: (0,) * len(shape))


def dispatch_kernel(experts, ids_ref, gates_ref, grad_ref, send_ref, rank_ref, main_ref, tail_ref, main_gate, tail_gate, tail_sum):
    step = pl.program_id(0)
    choices, tokens = ids_ref.shape
    rows = experts * MAIN

    @pl.when(step == 0)
    def _():
        expert = iota((experts, tokens), 0)
        hit = jnp.zeros((experts, tokens), F32)
        gate = jnp.zeros((experts, tokens), F32)
        for k in range(choices):
            same = ids_ref[k : k + 1, :] == expert
            hit = jnp.where(same, 1.0, hit)
            gate = jnp.where(same, gates_ref[k : k + 1, :], gate)
        earlier = (iota((tokens, tokens), 0) < iota((tokens, tokens), 1)).astype(F32).astype(BF16)
        rank = jnp.where(hit > 0.0, plain_dot(hit.astype(BF16), earlier), -1.0)
        rank_ref[...] = rank
        position = iota((experts, MAIN, tokens), 1)
        spread_rank = jnp.broadcast_to(rank[:, None, :], (experts, MAIN, tokens))
        spread_gate = jnp.broadcast_to(gate[:, None, :], (experts, MAIN, tokens))
        for wanted, pick_ref, scale_ref in (
            (position, main_ref, main_gate),
            (MAIN + (position >> 3), tail_ref, tail_gate),
        ):
            taken = spread_rank == wanted.astype(F32)
            pick_ref[...] = jnp.where(taken, 1.0, 0.0).reshape(rows, tokens).astype(BF16)
            scale = jnp.where(taken, spread_gate, 0.0).reshape(rows, tokens)
            scale_ref[...] = jnp.sum(scale, axis=1, keepdims=True)
        tail_sum[...] = jnp.zeros_like(tail_sum)

    width = grad_ref.shape[1]

    @pl.when(step < CUTS)
    def _():
        grad = grad_ref[...]
        picked = plain_dot(main_ref[...], grad) * main_gate[...]
        send_ref[...] = picked.astype(BF16).reshape(experts, MAIN, width)
        mine = (iota((rows, width), 0) & (CUTS - 1)) == step
        tail_sum[...] = jnp.where(mine, plain_dot(tail_ref[...], grad), tail_sum[...])

    @pl.when(step == CUTS)
    def _():
        send_ref[...] = (tail_sum[...] * tail_gate[...]).astype(BF16).reshape(experts, MAIN, width)


def dispatch(ids, gates, grad, experts):
    choices, tokens = ids.shape
    model = grad.shape[1]
    width = model // CUTS
    rows = experts * MAIN
    return pl.pallas_call(
        functools.partial(dispatch_kernel, experts),
        grid=(CUTS + 1,),
        in_specs=[
            whole((choices, tokens)),
            whole((choices, tokens)),
            pl.BlockSpec((tokens, width), lambda step: (0, jnp.minimum(step, CUTS - 1))),
        ],
        out_specs=[
            pl.BlockSpec((experts, MAIN, width), lambda step: (0, 0, step)),
            whole((experts, tokens)),
        ],
        out_shape=[
            jax.ShapeDtypeStruct((experts, MAIN, model + width), BF16),
            jax.ShapeDtypeStruct((experts, tokens), F32),
        ],
        scratch_shapes=[
            pltpu.VMEM((rows, tokens), BF16),
            pltpu.VMEM((rows, tokens), BF16),
            pltpu.VMEM((rows, 1), F32),
            pltpu.VMEM((rows, 1), F32),
            pltpu.VMEM((rows, width), F32),
        ],
        compiler_params=pltpu.CompilerParams(vmem_limit_bytes=32 << 20),
        cost_estimate=pl.CostEstimate(
            flops=4 * rows * tokens * model, bytes_accessed=2 * (tokens + rows) * model, transcendentals=0
        ),
        name="dispatch",
    )(ids, gates, grad)


def slot_row(index, experts):
    source, rank = index >> 4, index & (MAIN - 1)
    main = jnp.where(rank < CAP, source * CAP + rank, experts * CAP + source * OC)
    left = index - experts * MAIN
    tail = experts * CAP + (left >> 1) * OC + 1 + (left & 1)
    return jnp.where(index < experts * MAIN, main, tail)


def travel_kernel(experts, own_ref, spill_ref, out_ref, home_pick, spill_pick):
    @pl.when(pl.program_id(0) == 0)
    def _():
        for pick, first in ((home_pick, 0), (spill_pick, experts * CAP)):
            same = slot_row(iota(pick.shape, 0), experts) == first + iota(pick.shape, 1)
            pick[...] = jnp.where(same, 1.0, 0.0).astype(BF16)

    out = plain_dot(home_pick[...], own_ref[...]) + plain_dot(spill_pick[...], spill_ref[...])
    out_ref[...] = out.astype(BF16)


def to_travel_order(own, spill, experts):
    slots, columns = own.shape
    width = columns // 3
    home, rest = experts * CAP, experts * OC
    return pl.pallas_call(
        functools.partial(travel_kernel, experts),
        grid=(3,),
        in_specs=[
            pl.BlockSpec((home, width), lambda step: (0, step)),
            pl.BlockSpec((rest, width), lambda step: (0, step)),
        ],
        out_specs=pl.BlockSpec((slots, width), lambda step: (0, step)),
        out_shape=jax.ShapeDtypeStruct((slots, columns), BF16),
        scratch_shapes=[pltpu.VMEM((slots, home), BF16), pltpu.VMEM((slots, rest), BF16)],
        compiler_params=pltpu.CompilerParams(vmem_limit_bytes=16 << 20),
        cost_estimate=pl.CostEstimate(
            flops=2 * slots * slots * columns, bytes_accessed=4 * slots * columns, transcendentals=0
        ),
        name="to_travel",
    )(own, spill)


def slots_kernel(experts, rows_ref, out_ref, pick):
    @pl.when(pl.program_id(0) == 0)
    def _():
        same = slot_row(iota(pick.shape, 1), experts) == iota(pick.shape, 0)
        pick[...] = jnp.where(same, 1.0, 0.0).astype(BF16)

    out_ref[...] = plain_dot(pick[...], rows_ref[...]).astype(BF16)


def to_slot_order(rows, experts):
    slots, columns = rows.shape
    width = columns // 3
    return pl.pallas_call(
        functools.partial(slots_kernel, experts),
        grid=(3,),
        in_specs=[pl.BlockSpec((slots, width), lambda step: (0, step))],
        out_specs=pl.BlockSpec((slots, width), lambda step: (0, step)),
        out_shape=jax.ShapeDtypeStruct((slots, columns), BF16),
        scratch_shapes=[pltpu.VMEM((slots, slots), BF16)],
        compiler_params=pltpu.CompilerParams(vmem_limit_bytes=16 << 20),
        cost_estimate=pl.CostEstimate(
            flops=2 * slots * slots * columns, bytes_accessed=4 * slots * columns, transcendentals=0
        ),
        name="to_slots",
    )(rows)


def hidden_kernel(experts, main_ref, tail_ref, down_ref, gate_ref, up_ref, out_gate_ref, out_up_ref, rows_ref):
    model = down_ref.shape[1]
    width = model // CUTS
    full = experts * MAIN
    left = experts * 2

    @pl.when(pl.program_id(0) == 0)
    def _():
        rows_ref[pl.ds(0, full), :] = main_ref[...].reshape(full, model)
        tail = tail_ref[...].reshape(full, width)
        row, lane = iota((left, full), 0), iota((left, full), 1)
        for cut in range(CUTS):
            pick = jnp.where(lane == row * CUTS + cut, 1.0, 0.0).astype(BF16)
            rows_ref[pl.ds(full, left), pl.ds(cut * width, width)] = plain_dot(pick, tail).astype(BF16)

    hidden_cot = rows_dot(rows_ref[...], down_ref[...])
    gate = gate_ref[...].astype(F32)
    up = up_ref[...].astype(F32)
    sigma = jax.nn.sigmoid(gate)
    out_gate_ref[...] = (hidden_cot * up * sigma * (1.0 + gate * (1.0 - sigma))).astype(BF16)
    out_up_ref[...] = (hidden_cot * gate * sigma).astype(BF16)


def hidden_pass(arrived, down, pre_acts):
    experts = arrived.shape[0]
    hidden, model = down.shape
    slots = pre_acts.shape[0]
    parts = 3
    width = hidden // parts
    return pl.pallas_call(
        functools.partial(hidden_kernel, experts),
        grid=(parts,),
        in_specs=[
            pl.BlockSpec((experts, MAIN, model), lambda step: (0, 0, 0)),
            pl.BlockSpec((experts, MAIN, model // CUTS), lambda step: (0, 0, CUTS)),
            pl.BlockSpec((width, model), lambda step: (step, 0)),
            pl.BlockSpec((slots, width), lambda step: (0, step)),
            pl.BlockSpec((slots, width), lambda step: (0, parts + step)),
        ],
        out_specs=[pl.BlockSpec((slots, width), lambda step: (0, step))] * 2,
        out_shape=[jax.ShapeDtypeStruct((slots, hidden), BF16)] * 2,
        scratch_shapes=[pltpu.VMEM((slots, model), BF16)],
        compiler_params=pltpu.CompilerParams(vmem_limit_bytes=40 << 20),
        cost_estimate=pl.CostEstimate(
            flops=2 * slots * hidden * model,
            bytes_accessed=2 * (slots * model + hidden * model + 4 * slots * hidden),
            transcendentals=slots * hidden,
        ),
        name="hidden",
    )(arrived, arrived, down, pre_acts, pre_acts)


def back_kernel(experts, gate_ref, up_ref, weight_ref, out_ref, tail_sum):
    step = pl.program_id(0)
    full = experts * MAIN
    left = experts * 2
    width = weight_ref.shape[0]
    hidden = gate_ref.shape[1]

    @pl.when(step == 0)
    def _():
        tail_sum[...] = jnp.zeros_like(tail_sum)

    @pl.when(step < CUTS)
    def _():
        back = rows_dot(gate_ref[...], weight_ref[:, :hidden]) + rows_dot(up_ref[...], weight_ref[:, hidden:])
        back = back.astype(BF16)
        out_ref[...] = back[:full].reshape(experts, MAIN, width)
        spread = jnp.where((iota((full, left), 0) >> 3) == iota((full, left), 1), 1.0, 0.0).astype(BF16)
        mine = (iota((full, width), 0) & (CUTS - 1)) == step
        tail_sum[...] = jnp.where(mine, plain_dot(spread, back[full:]), tail_sum[...])

    @pl.when(step == CUTS)
    def _():
        out_ref[...] = tail_sum[...].astype(BF16).reshape(experts, MAIN, width)


def back_pass(gate_grad, up_grad, weight, experts):
    slots, hidden = gate_grad.shape
    model = weight.shape[0]
    width = model // CUTS
    return pl.pallas_call(
        functools.partial(back_kernel, experts),
        grid=(CUTS + 1,),
        in_specs=[
            whole((slots, hidden)),
            whole((slots, hidden)),
            pl.BlockSpec((width, 2 * hidden), lambda step: (jnp.minimum(step, CUTS - 1), 0)),
        ],
        out_specs=pl.BlockSpec((experts, MAIN, width), lambda step: (0, 0, step)),
        out_shape=jax.ShapeDtypeStruct((experts, MAIN, model + width), BF16),
        scratch_shapes=[pltpu.VMEM((experts * MAIN, width), F32)],
        compiler_params=pltpu.CompilerParams(vmem_limit_bytes=32 << 20),
        cost_estimate=pl.CostEstimate(
            flops=4 * slots * hidden * model,
            bytes_accessed=2 * (slots * model + 2 * hidden * model + 2 * slots * hidden),
            transcendentals=0,
        ),
        name="back",
    )(gate_grad, up_grad, weight)


def combine_kernel(experts, rank_ref, main_ref, tail_ref, out_ref, pick, spread):
    step = pl.program_id(0)
    tokens = rank_ref.shape[1]
    full = experts * MAIN
    width = out_ref.shape[1]

    @pl.when(step == 0)
    def _():
        same = jnp.where(iota((tokens, tokens), 0) == iota((tokens, tokens), 1), 1.0, 0.0).astype(BF16)
        by_token = rows_dot(same, rank_ref[...].astype(BF16)).astype(BF16)
        widen = jnp.where((iota((experts, full), 1) >> 4) == iota((experts, full), 0), 1.0, 0.0).astype(BF16)
        spread[...] = plain_dot(by_token, widen)
        place = (iota((tokens, full), 1) & (MAIN - 1)).astype(F32)
        pick[...] = jnp.where(spread[...] == place, 1.0, 0.0).astype(BF16)

    lane = iota((tokens, full), 1)
    place = (MAIN + ((lane >> 3) & 1)).astype(F32)
    mine = (spread[...] == place) & ((lane & (CUTS - 1)) == step)
    total = plain_dot(pick[...], main_ref[...].reshape(full, width))
    total += plain_dot(jnp.where(mine, 1.0, 0.0).astype(BF16), tail_ref[...].reshape(full, width))
    out_ref[...] = total.astype(BF16)


def combine(rank, returned):
    experts, tokens = rank.shape
    width = returned.shape[2] // (CUTS + 1)
    model = width * CUTS
    full = experts * MAIN
    return pl.pallas_call(
        functools.partial(combine_kernel, experts),
        grid=(CUTS,),
        in_specs=[
            whole((experts, tokens)),
            pl.BlockSpec((experts, MAIN, width), lambda step: (0, 0, step)),
            pl.BlockSpec((experts, MAIN, width), lambda step: (0, 0, CUTS)),
        ],
        out_specs=pl.BlockSpec((tokens, width), lambda step: (0, step)),
        out_shape=jax.ShapeDtypeStruct((tokens, model), BF16),
        scratch_shapes=[pltpu.VMEM((tokens, full), BF16), pltpu.VMEM((tokens, full), F32)],
        compiler_params=pltpu.CompilerParams(vmem_limit_bytes=32 << 20),
        cost_estimate=pl.CostEstimate(
            flops=4 * full * tokens * model, bytes_accessed=2 * (tokens + full) * model, transcendentals=0
        ),
        name="combine",
    )(rank, returned, returned)


def moved(rows, offset, sign):
    replicas = lax.axis_size("dp")
    for bit in range(replicas.bit_length() - 1):
        by = sign * (1 << bit)
        shifted = lax.ppermute(rows, "dp", [(i, (i + by) % replicas) for i in range(replicas)])
        rows = jnp.where(offset >> bit & 1 == 1, shifted, rows)
    return rows


def exchange(blocks):
    return lax.all_to_all(blocks, "expert", split_axis=0, concat_axis=0, tiled=True)


def body(out_grad, route_gates, expert_ids, partner_offset, saved_pre, down_weight, gate_up_weight):
    experts = lax.axis_size("expert")
    home = experts * CAP
    offset = partner_offset[0]
    own_pre = saved_pre[0, 0]
    down = lax.all_gather(down_weight[0], "dp", axis=1, tiled=True)
    gate_up = lax.all_gather(gate_up_weight[0], "dp", axis=0, tiled=True)
    sent, rank = dispatch(expert_ids.T, route_gates.T, out_grad, experts)
    arrived = exchange(sent)
    spill_pre = moved(own_pre[home:], offset, -1)
    pre_acts = to_travel_order(own_pre, spill_pre, experts)
    gate_grad, up_grad = hidden_pass(arrived, down, pre_acts)
    back = back_pass(gate_grad, up_grad, gate_up, experts)
    returned = exchange(back)
    by_slot = to_slot_order(jnp.concatenate([gate_grad, up_grad], 1), experts)
    spill_grad = moved(by_slot[home:], offset, 1)
    hidden_grad = lax.dynamic_update_slice(by_slot, spill_grad, (home, 0))
    token_grad = combine(rank, returned)
    return token_grad, hidden_grad.reshape(saved_pre.shape)


def solution(mesh):
    placed = (
        P(("dp", "expert"), None),
        P(("dp", "expert"), None),
        P(("dp", "expert"), None),
        P("expert"),
        P("dp", "expert", None, None),
        P("expert", None, "dp"),
        P("expert", "dp", None),
    )
    return jax.shard_map(
        body,
        mesh=mesh,
        in_specs=placed,
        out_specs=(P(("dp", "expert"), None), P("dp", "expert", None, None)),
        check_vma=False,
    )
```

```python
import functools

import jax
import jax.numpy as jnp
from jax import lax
from jax.experimental import pallas as pl
from jax.experimental.pallas import tpu as pltpu
from jax.sharding import PartitionSpec as P

CAP = 15
OC = 3
MAIN = 16
CUTS = 8
F32 = jnp.float32
BF16 = jnp.bfloat16


def iota(shape, axis):
    return lax.broadcasted_iota(jnp.int32, shape, axis)


def rows_dot(left, right):
    return lax.dot_general(left, right, (((1,), (1,)), ((), ())), preferred_element_type=F32)


def plain_dot(left, right):
    return lax.dot_general(left, right, (((1,), (0,)), ((), ())), preferred_element_type=F32)


def whole(shape):
    return pl.BlockSpec(shape, lambda step: (0,) * len(shape))


def piece_rows(shape, travel_axis, left):
    travelling, by_piece = iota(shape, travel_axis), iota(shape, 1 - travel_axis)
    same = travelling == ((by_piece & (left - 1)) << 3) + (by_piece >> (left.bit_length() - 1))
    return jnp.where(same, 1.0, 0.0).astype(BF16)


def anywhere():
    return pl.BlockSpec(memory_space=pl.ANY)


def in_vmem():
    return pl.BlockSpec(memory_space=pltpu.VMEM)


def columns(cut, width):
    return pl.ds(pl.multiple_of(cut * width, width), width)


def dispatch_kernel(
    experts, ids_ref, gates_ref, grad_ref, send_ref, rank_ref, main_pick, tail_pick, main_gate, tail_gate, stage, pieces, sems
):
    choices, tokens = ids_ref.shape
    full, left = experts * MAIN, experts * 2
    width = grad_ref.shape[1] // CUTS
    expert = iota((experts, tokens), 0)
    hit = jnp.zeros((experts, tokens), F32)
    gate = jnp.zeros((experts, tokens), F32)
    for k in range(choices):
        same = ids_ref[k : k + 1, :] == expert
        hit = jnp.where(same, 1.0, hit)
        gate = jnp.where(same, gates_ref[k : k + 1, :], gate)
    earlier = (iota((tokens, tokens), 0) < iota((tokens, tokens), 1)).astype(F32).astype(BF16)
    rank = jnp.where(hit > 0.0, plain_dot(hit.astype(BF16), earlier), -1.0)
    rank_ref[...] = rank
    for deep, first, pick_ref, scale_ref in ((MAIN, 0, main_pick, main_gate), (8, MAIN, tail_pick, tail_gate)):
        position = iota((experts, deep, tokens), 1)
        wanted = (first + position).astype(F32)
        taken = jnp.broadcast_to(rank[:, None, :], wanted.shape) == wanted
        scale = jnp.where(taken, jnp.broadcast_to(gate[:, None, :], wanted.shape), 0.0)
        one = jnp.where(taken, 1.0, 0.0)
        if deep == MAIN:
            pick_ref[...] = one.reshape(full, tokens).astype(BF16)
            scale_ref[...] = jnp.sum(scale.reshape(full, tokens), axis=1, keepdims=True)
        else:
            row = iota((left, experts * deep), 0)
            keep = iota((left, experts * deep), 1) == ((row >> 1) << 3) + (row & 1)
            keep = jnp.where(keep, 1.0, 0.0)
            pick_ref[...] = plain_dot(keep.astype(BF16), one.reshape(experts * deep, tokens).astype(BF16)).astype(BF16)
            by_row = rows_by(gate, left)
            scale_ref[...] = jnp.sum(jnp.where(pick_ref[...].astype(F32) > 0.0, by_row, 0.0), axis=1, keepdims=True)

    def one_cut(cut, carry):
        grad = grad_ref[:, columns(cut, width)]
        picked = plain_dot(main_pick[...], grad) * main_gate[...]
        stage[cut] = picked.astype(BF16)
        pltpu.make_async_copy(stage.at[cut], send_ref.at[:, columns(cut, width)], sems.at[cut]).start()
        pieces[cut] = (plain_dot(tail_pick[...], grad) * tail_gate[...]).astype(BF16)
        return carry

    lax.fori_loop(0, CUTS, one_cut, 0)
    stage[CUTS] = plain_dot(piece_rows((full, full), 0, left), pieces[...].reshape(full, width)).astype(BF16)
    pltpu.make_async_copy(stage.at[CUTS], send_ref.at[:, columns(CUTS, width)], sems.at[CUTS]).start()

    def finish(cut, carry):
        pltpu.make_async_copy(stage.at[cut], send_ref.at[:, columns(cut, width)], sems.at[cut]).wait()
        return carry

    lax.fori_loop(0, CUTS + 1, finish, 0)


def rows_by(values, rows):
    n, m = values.shape
    return jnp.broadcast_to(values[:, None, :], (n, rows // n, m)).reshape(rows, m)


def dispatch(ids, gates, grad, experts):
    choices, tokens = ids.shape
    model = grad.shape[1]
    width = model // CUTS
    full, left = experts * MAIN, experts * 2
    return pl.pallas_call(
        functools.partial(dispatch_kernel, experts),
        in_specs=[in_vmem()] * 3,
        out_specs=[anywhere(), in_vmem()],
        out_shape=[
            jax.ShapeDtypeStruct((full, model + width), BF16),
            jax.ShapeDtypeStruct((experts, tokens), F32),
        ],
        scratch_shapes=[
            pltpu.VMEM((full, tokens), BF16),
            pltpu.VMEM((left, tokens), BF16),
            pltpu.VMEM((full, 1), F32),
            pltpu.VMEM((left, 1), F32),
            pltpu.VMEM((CUTS + 1, full, width), BF16),
            pltpu.VMEM((CUTS, left, width), BF16),
            pltpu.SemaphoreType.DMA((CUTS + 1,)),
        ],
        compiler_params=pltpu.CompilerParams(vmem_limit_bytes=56 << 20),
        cost_estimate=pl.CostEstimate(
            flops=2 * full * tokens * model, bytes_accessed=2 * (tokens + full) * model, transcendentals=0
        ),
        name="dispatch",
    )(ids, gates, grad)


def slot_row(index, experts):
    source, rank = index >> 4, index & (MAIN - 1)
    main = jnp.where(rank < CAP, source * CAP + rank, experts * CAP + source * OC)
    left = index - experts * MAIN
    tail = experts * CAP + (left >> 1) * OC + 1 + (left & 1)
    return jnp.where(index < experts * MAIN, main, tail)


def travel_kernel(experts, rank_ref, own_ref, spill_ref, out_ref, place_ref, home_pick, spill_pick):
    @pl.when(pl.program_id(0) == 0)
    def _():
        for pick, first in ((home_pick, 0), (spill_pick, experts * CAP)):
            same = slot_row(iota(pick.shape, 0), experts) == first + iota(pick.shape, 1)
            pick[...] = jnp.where(same, 1.0, 0.0).astype(BF16)
        tokens, slots = place_ref.shape
        same = jnp.where(iota((tokens, tokens), 0) == iota((tokens, tokens), 1), 1.0, 0.0).astype(BF16)
        by_token = rows_dot(same, rank_ref[...].astype(BF16)).astype(BF16)
        full = experts * MAIN

        def named(shape):
            lane = iota(shape, 1)
            left = lane - full
            of = jnp.where(lane < full, lane >> 4, left >> 1)
            at = jnp.where(lane < full, lane & (MAIN - 1), MAIN + (left & 1))
            return of, at

        of, _ = named((experts, slots))
        widen = jnp.where(of == iota((experts, slots), 0), 1.0, 0.0).astype(BF16)
        _, at = named((tokens, slots))
        place_ref[...] = jnp.where(plain_dot(by_token, widen) == at.astype(F32), 1.0, 0.0).astype(BF16)

    out = plain_dot(home_pick[...], own_ref[...]) + plain_dot(spill_pick[...], spill_ref[...])
    out_ref[...] = out.astype(BF16)


def to_travel_order(rank, own, spill, experts):
    slots, columns = own.shape
    tokens = rank.shape[1]
    width = columns // 3
    home, rest = experts * CAP, experts * OC
    return pl.pallas_call(
        functools.partial(travel_kernel, experts),
        grid=(3,),
        in_specs=[
            whole((experts, tokens)),
            pl.BlockSpec((home, width), lambda step: (0, step)),
            pl.BlockSpec((rest, width), lambda step: (0, step)),
        ],
        out_specs=[pl.BlockSpec((slots, width), lambda step: (0, step)), whole((tokens, slots))],
        out_shape=[jax.ShapeDtypeStruct((slots, columns), BF16), jax.ShapeDtypeStruct((tokens, slots), BF16)],
        scratch_shapes=[pltpu.VMEM((slots, home), BF16), pltpu.VMEM((slots, rest), BF16)],
        compiler_params=pltpu.CompilerParams(vmem_limit_bytes=16 << 20),
        cost_estimate=pl.CostEstimate(
            flops=2 * slots * slots * columns, bytes_accessed=4 * slots * columns, transcendentals=0
        ),
        name="to_travel",
    )(rank, own, spill)


def slots_kernel(experts, rows_ref, out_ref, pick):
    @pl.when(pl.program_id(0) == 0)
    def _():
        same = slot_row(iota(pick.shape, 1), experts) == iota(pick.shape, 0)
        pick[...] = jnp.where(same, 1.0, 0.0).astype(BF16)

    out_ref[...] = plain_dot(pick[...], rows_ref[...]).astype(BF16)


def to_slot_order(rows, experts):
    slots, columns = rows.shape
    width = columns // 3
    return pl.pallas_call(
        functools.partial(slots_kernel, experts),
        grid=(3,),
        in_specs=[pl.BlockSpec((slots, width), lambda step: (0, step))],
        out_specs=pl.BlockSpec((slots, width), lambda step: (0, step)),
        out_shape=jax.ShapeDtypeStruct((slots, columns), BF16),
        scratch_shapes=[pltpu.VMEM((slots, slots), BF16)],
        compiler_params=pltpu.CompilerParams(vmem_limit_bytes=16 << 20),
        cost_estimate=pl.CostEstimate(
            flops=2 * slots * slots * columns, bytes_accessed=4 * slots * columns, transcendentals=0
        ),
        name="to_slots",
    )(rows)


def expert_kernel(experts, *refs):
    where_ref, arrived, pre_ref = refs[:3]
    downs, gate_ups = refs[3 : 3 + CUTS], refs[3 + CUTS : 3 + 2 * CUTS]
    grad_ref, back_ref = refs[3 + 2 * CUTS : 5 + 2 * CUTS]
    rows, tail, pieces, down, gate_up, total, stage, row_sem, down_sem, up_sem, out_sem = refs[5 + 2 * CUTS :]
    full, left = experts * MAIN, experts * 2
    hidden, width = down.shape[1:]

    def rows_copy(k):
        return pltpu.make_async_copy(
            arrived.at[:, columns(where_ref[k], width)], rows.at[k, pl.ds(0, full)], row_sem.at[k]
        )

    def out_copy(k, cut):
        return pltpu.make_async_copy(stage.at[k], back_ref.at[:, columns(cut, width)], out_sem.at[k])

    tail_copy = pltpu.make_async_copy(arrived.at[:, columns(CUTS, width)], tail, row_sem.at[CUTS])
    tail_copy.start()
    for k in range(CUTS):
        rows_copy(k).start()
        pltpu.make_async_copy(downs[k], down.at[k], down_sem.at[k]).start()
    for k in range(CUTS):
        pltpu.make_async_copy(gate_ups[k], gate_up.at[k], up_sem.at[k]).start()
    total[...] = jnp.zeros_like(total)
    order = piece_rows((full, full), 1, left)
    tail_copy.wait()
    pieces[...] = plain_dot(order, tail[...]).astype(BF16).reshape(CUTS, left, width)

    def first_product(k, carry):
        rows_copy(k).wait()
        pltpu.make_async_copy(downs[0], down.at[k], down_sem.at[k]).wait()
        rows[k, pl.ds(full, left)] = pieces[where_ref[k]]
        total[...] += rows_dot(rows[k], down[k])
        return carry

    lax.fori_loop(0, CUTS, first_product, 0)
    part = hidden // 3
    for n in range(3):
        own, other = pl.ds(n * part, part), pl.ds(hidden + n * part, part)
        hidden_cot = total[:, own]
        gate = pre_ref[:, own].astype(F32)
        up = pre_ref[:, other].astype(F32)
        sigma = jax.nn.sigmoid(gate)
        grad_ref[:, own] = (hidden_cot * up * sigma * (1.0 + gate * (1.0 - sigma))).astype(BF16)
        grad_ref[:, other] = (hidden_cot * gate * sigma).astype(BF16)

    def second_product(k, carry):
        pltpu.make_async_copy(gate_ups[0], gate_up.at[k], up_sem.at[k]).wait()
        back = rows_dot(grad_ref[...], gate_up[k]).astype(BF16)
        stage[k] = back[:full]
        pieces[where_ref[k]] = back[full:]
        out_copy(k, where_ref[k]).start()
        return carry

    lax.fori_loop(0, CUTS, second_product, 0)
    order = piece_rows((full, full), 0, left)
    stage[CUTS] = plain_dot(order, pieces[...].reshape(full, width)).astype(BF16)
    out_copy(CUTS, CUTS).start()

    def finish(k, carry):
        out_copy(k, where_ref[k]).wait()
        return carry

    lax.fori_loop(0, CUTS, finish, 0)
    out_copy(CUTS, CUTS).wait()


def expert_pass(where, arrived, pre_acts, downs, gate_ups):
    full, length = arrived.shape
    hidden, width = downs[0].shape
    slots, both = pre_acts.shape
    model = length - width
    experts = full // MAIN
    left = experts * 2
    return pl.pallas_call(
        functools.partial(expert_kernel, experts),
        in_specs=[pl.BlockSpec(memory_space=pltpu.SMEM), anywhere(), in_vmem()] + [anywhere()] * (2 * CUTS),
        out_specs=[in_vmem(), anywhere()],
        out_shape=[jax.ShapeDtypeStruct((slots, both), BF16), jax.ShapeDtypeStruct((full, length), BF16)],
        scratch_shapes=[
            pltpu.VMEM((CUTS, slots, width), BF16),
            pltpu.VMEM((full, width), BF16),
            pltpu.VMEM((CUTS, left, width), BF16),
            pltpu.VMEM((CUTS, hidden, width), BF16),
            pltpu.VMEM((CUTS, width, both), BF16),
            pltpu.VMEM((slots, hidden), F32),
            pltpu.VMEM((CUTS + 1, full, width), BF16),
            pltpu.SemaphoreType.DMA((CUTS + 1,)),
            pltpu.SemaphoreType.DMA((CUTS,)),
            pltpu.SemaphoreType.DMA((CUTS,)),
            pltpu.SemaphoreType.DMA((CUTS + 1,)),
        ],
        compiler_params=pltpu.CompilerParams(vmem_limit_bytes=56 << 20),
        cost_estimate=pl.CostEstimate(
            flops=6 * slots * hidden * model,
            bytes_accessed=2 * (2 * slots * model + 3 * hidden * model + 2 * slots * both),
            transcendentals=slots * hidden,
        ),
        name="experts",
    )(where, arrived, pre_acts, *downs, *gate_ups)


def combine_kernel(place_ref, main_ref, tail_ref, out_ref, pieces):
    step = pl.program_id(0)
    full, width = tail_ref.shape
    left = pieces.shape[1]

    @pl.when(step == 0)
    def _():
        order = piece_rows((full, full), 1, left)
        pieces[...] = plain_dot(order, tail_ref[...]).astype(BF16).reshape(CUTS, left, width)

    for half in range(2):
        part = pl.ds(half * width, width)
        total = plain_dot(place_ref[:, :full], main_ref[:, part])
        total += plain_dot(place_ref[:, full:], pieces[2 * step + half])
        out_ref[:, part] = total.astype(BF16)


def combine(place, returned):
    full, length = returned.shape
    tokens, slots = place.shape
    width = length // (CUTS + 1)
    model = width * CUTS
    left = slots - full
    return pl.pallas_call(
        combine_kernel,
        grid=(CUTS // 2,),
        in_specs=[
            whole((tokens, slots)),
            pl.BlockSpec((full, 2 * width), lambda step: (0, step)),
            pl.BlockSpec((full, width), lambda step: (0, CUTS)),
        ],
        out_specs=pl.BlockSpec((tokens, 2 * width), lambda step: (0, step)),
        out_shape=jax.ShapeDtypeStruct((tokens, model), BF16),
        scratch_shapes=[pltpu.VMEM((CUTS, left, width), BF16)],
        compiler_params=pltpu.CompilerParams(vmem_limit_bytes=56 << 20),
        cost_estimate=pl.CostEstimate(
            flops=2 * slots * tokens * model, bytes_accessed=2 * (tokens + slots) * model, transcendentals=0
        ),
        name="combine",
    )(place, returned, returned)


def along_dp(shard, target):
    return lax.ppermute(shard, "dp", [(i, target(i)) for i in range(lax.axis_size("dp"))])


def gathered(shard):
    count = lax.axis_size("dp")
    core = lax.axis_index("dp") & 1
    below = along_dp(shard, lambda i: (i + 2) % count)
    above = along_dp(shard, lambda i: (i - 2) % count)
    across = along_dp(jnp.where(core == 0, below, above), lambda i: (i + 2 - 4 * (i & 1)) % count)
    held = [shard, below, above, across]
    return held + [along_dp(part, lambda i: i ^ 1) for part in held]


def shard_places():
    count = lax.axis_size("dp")
    me = lax.axis_index("dp")
    steps = jnp.array([0, -2, 2, 4], jnp.int32)
    return jnp.concatenate([(me + steps + count) % count, ((me ^ 1) + steps + count) % count]).astype(jnp.int32)


def moved(rows, offset, sign):
    replicas = lax.axis_size("dp")
    for bit in range(replicas.bit_length() - 1):
        by = sign * (1 << bit)
        shifted = lax.ppermute(rows, "dp", [(i, (i + by) % replicas) for i in range(replicas)])
        rows = jnp.where(offset >> bit & 1 == 1, shifted, rows)
    return rows


def exchange(rows, experts):
    blocks = rows.reshape(experts, MAIN, rows.shape[1])
    return lax.all_to_all(blocks, "expert", split_axis=0, concat_axis=0, tiled=True).reshape(rows.shape)


def body(out_grad, route_gates, expert_ids, partner_offset, saved_pre, down_weight, gate_up_weight):
    experts = lax.axis_size("expert")
    home = experts * CAP
    offset = partner_offset[0]
    own_pre = saved_pre[0, 0]
    sent, rank = dispatch(expert_ids.T, route_gates.T, out_grad, experts)
    arrived = exchange(sent, experts)
    downs, gate_ups = gathered(down_weight[0]), gathered(gate_up_weight[0])
    spill_pre = moved(own_pre[home:], offset, -1)
    pre_acts, place = to_travel_order(rank, own_pre, spill_pre, experts)
    travel_grad, back = expert_pass(shard_places(), arrived, pre_acts, downs, gate_ups)
    returned = exchange(back, experts)
    by_slot = to_slot_order(travel_grad, experts)
    spill_grad = moved(by_slot[home:], offset, 1)
    hidden_grad = lax.dynamic_update_slice(by_slot, spill_grad, (home, 0))
    token_grad = combine(place, returned)
    return token_grad, hidden_grad.reshape(saved_pre.shape)


def solution(mesh):
    placed = (
        P(("dp", "expert"), None),
        P(("dp", "expert"), None),
        P(("dp", "expert"), None),
        P("expert"),
        P("dp", "expert", None, None),
        P("expert", None, "dp"),
        P("expert", "dp", None),
    )
    return jax.shard_map(
        body,
        mesh=mesh,
        in_specs=placed,
        out_specs=(P(("dp", "expert"), None), P("dp", "expert", None, None)),
        check_vma=False,
    )
```

```python
import functools

import jax
import jax.numpy as jnp
from jax import lax
from jax.experimental import pallas as pl
from jax.experimental.pallas import tpu as pltpu
from jax.sharding import PartitionSpec as P

CAP = 15
OC = 3
MAIN = 16
CUTS = 8
F32 = jnp.float32
BF16 = jnp.bfloat16


def iota(shape, axis):
    return lax.broadcasted_iota(jnp.int32, shape, axis)


def rows_dot(left, right):
    return lax.dot_general(left, right, (((1,), (1,)), ((), ())), preferred_element_type=F32)


def plain_dot(left, right):
    return lax.dot_general(left, right, (((1,), (0,)), ((), ())), preferred_element_type=F32)


def whole(shape):
    return pl.BlockSpec(shape, lambda step: (0,) * len(shape))


def piece_rows(shape, travel_axis, left):
    travelling, by_piece = iota(shape, travel_axis), iota(shape, 1 - travel_axis)
    same = travelling == ((by_piece & (left - 1)) << 3) + (by_piece >> (left.bit_length() - 1))
    return jnp.where(same, 1.0, 0.0).astype(BF16)


def anywhere():
    return pl.BlockSpec(memory_space=pl.ANY)


def in_vmem():
    return pl.BlockSpec(memory_space=pltpu.VMEM)


def columns(cut, width):
    return pl.ds(pl.multiple_of(cut * width, width), width)


def dispatch_kernel(
    experts, ids_ref, gates_ref, grad_ref, send_ref, rank_ref, main_pick, tail_pick, main_gate, tail_gate, grads, stage, pieces, grad_sem, sems
):
    choices, tokens = ids_ref.shape
    full, left = experts * MAIN, experts * 2
    width = grads.shape[2]

    def grad_copy(cut):
        return pltpu.make_async_copy(grad_ref.at[:, pl.ds(cut * width, width)], grads.at[cut], grad_sem.at[cut])

    def send_copy(cut):
        return pltpu.make_async_copy(stage.at[cut], send_ref.at[:, pl.ds(cut * width, width)], sems.at[cut])

    for cut in range(CUTS):
        grad_copy(cut).start()
    expert = iota((experts, tokens), 0)
    hit = jnp.zeros((experts, tokens), F32)
    gate = jnp.zeros((experts, tokens), F32)
    for k in range(choices):
        same = ids_ref[k : k + 1, :] == expert
        hit = jnp.where(same, 1.0, hit)
        gate = jnp.where(same, gates_ref[k : k + 1, :], gate)
    earlier = (iota((tokens, tokens), 0) < iota((tokens, tokens), 1)).astype(F32).astype(BF16)
    rank = jnp.where(hit > 0.0, plain_dot(hit.astype(BF16), earlier), -1.0)
    rank_ref[...] = rank
    for deep, first, pick_ref, scale_ref in ((MAIN, 0, main_pick, main_gate), (8, MAIN, tail_pick, tail_gate)):
        position = iota((experts, deep, tokens), 1)
        wanted = (first + position).astype(F32)
        taken = jnp.broadcast_to(rank[:, None, :], wanted.shape) == wanted
        scale = jnp.where(taken, jnp.broadcast_to(gate[:, None, :], wanted.shape), 0.0)
        one = jnp.where(taken, 1.0, 0.0)
        if deep == MAIN:
            pick_ref[...] = one.reshape(full, tokens).astype(BF16)
            scale_ref[...] = jnp.sum(scale.reshape(full, tokens), axis=1, keepdims=True)
        else:
            row = iota((left, experts * deep), 0)
            keep = iota((left, experts * deep), 1) == ((row >> 1) << 3) + (row & 1)
            keep = jnp.where(keep, 1.0, 0.0)
            pick_ref[...] = plain_dot(keep.astype(BF16), one.reshape(experts * deep, tokens).astype(BF16)).astype(BF16)
            by_row = rows_by(gate, left)
            scale_ref[...] = jnp.sum(jnp.where(pick_ref[...].astype(F32) > 0.0, by_row, 0.0), axis=1, keepdims=True)

    for cut in range(CUTS):
        grad_copy(cut).wait()
        grad = grads[cut]
        stage[cut] = (plain_dot(main_pick[...], grad) * main_gate[...]).astype(BF16)
        send_copy(cut).start()
        pieces[cut] = (plain_dot(tail_pick[...], grad) * tail_gate[...]).astype(BF16)
    stage[CUTS] = plain_dot(piece_rows((full, full), 0, left), pieces[...].reshape(full, width)).astype(BF16)
    send_copy(CUTS).start()
    for cut in range(CUTS + 1):
        send_copy(cut).wait()


def rows_by(values, rows):
    n, m = values.shape
    return jnp.broadcast_to(values[:, None, :], (n, rows // n, m)).reshape(rows, m)


def dispatch(ids, gates, grad, experts):
    choices, tokens = ids.shape
    model = grad.shape[1]
    width = model // CUTS
    full, left = experts * MAIN, experts * 2
    return pl.pallas_call(
        functools.partial(dispatch_kernel, experts),
        in_specs=[in_vmem(), in_vmem(), anywhere()],
        out_specs=[anywhere(), in_vmem()],
        out_shape=[
            jax.ShapeDtypeStruct((full, model + width), BF16),
            jax.ShapeDtypeStruct((experts, tokens), F32),
        ],
        scratch_shapes=[
            pltpu.VMEM((full, tokens), BF16),
            pltpu.VMEM((left, tokens), BF16),
            pltpu.VMEM((full, 1), F32),
            pltpu.VMEM((left, 1), F32),
            pltpu.VMEM((CUTS, tokens, width), BF16),
            pltpu.VMEM((CUTS + 1, full, width), BF16),
            pltpu.VMEM((CUTS, left, width), BF16),
            pltpu.SemaphoreType.DMA((CUTS,)),
            pltpu.SemaphoreType.DMA((CUTS + 1,)),
        ],
        compiler_params=pltpu.CompilerParams(vmem_limit_bytes=60 << 20),
        cost_estimate=pl.CostEstimate(
            flops=2 * full * tokens * model, bytes_accessed=2 * (tokens + full) * model, transcendentals=0
        ),
        name="dispatch",
    )(ids, gates, grad)


def slot_row(index, experts):
    source, rank = index >> 4, index & (MAIN - 1)
    main = jnp.where(rank < CAP, source * CAP + rank, experts * CAP + source * OC)
    left = index - experts * MAIN
    tail = experts * CAP + (left >> 1) * OC + 1 + (left & 1)
    return jnp.where(index < experts * MAIN, main, tail)


def travel_kernel(experts, rank_ref, *refs):
    pres, (gate_ref, up_ref, place_ref, home_pick, spill_pick) = refs[:4], refs[4:]

    @pl.when(pl.program_id(0) == 0)
    def _():
        for pick, first in ((home_pick, 0), (spill_pick, experts * CAP)):
            same = slot_row(iota(pick.shape, 0), experts) == first + iota(pick.shape, 1)
            pick[...] = jnp.where(same, 1.0, 0.0).astype(BF16)
        tokens, slots = place_ref.shape
        same = jnp.where(iota((tokens, tokens), 0) == iota((tokens, tokens), 1), 1.0, 0.0).astype(BF16)
        by_token = rows_dot(same, rank_ref[...].astype(BF16)).astype(BF16)
        full = experts * MAIN

        def named(shape):
            lane = iota(shape, 1)
            left = lane - full
            of = jnp.where(lane < full, lane >> 4, left >> 1)
            at = jnp.where(lane < full, lane & (MAIN - 1), MAIN + (left & 1))
            return of, at

        of, _ = named((experts, slots))
        widen = jnp.where(of == iota((experts, slots), 0), 1.0, 0.0).astype(BF16)
        _, at = named((tokens, slots))
        place_ref[...] = jnp.where(plain_dot(by_token, widen) == at.astype(F32), 1.0, 0.0).astype(BF16)

    gate, up = (
        plain_dot(home_pick[...], own[...]) + plain_dot(spill_pick[...], spill[...])
        for own, spill in (pres[:2], pres[2:])
    )
    sigma = jax.nn.sigmoid(gate)
    gate_ref[...] = up * sigma * (1.0 + gate * (1.0 - sigma))
    up_ref[...] = gate * sigma


def travel_factors(rank, own, spill, experts):
    slots = own.shape[0]
    tokens = rank.shape[1]
    hidden = own.shape[1] // 2
    parts = 3
    width = hidden // parts
    home, rest = experts * CAP, experts * OC
    gate_block, up_block = (lambda step: (0, step)), (lambda step: (0, parts + step))
    return pl.pallas_call(
        functools.partial(travel_kernel, experts),
        grid=(parts,),
        in_specs=[
            whole((experts, tokens)),
            pl.BlockSpec((home, width), gate_block),
            pl.BlockSpec((rest, width), gate_block),
            pl.BlockSpec((home, width), up_block),
            pl.BlockSpec((rest, width), up_block),
        ],
        out_specs=[pl.BlockSpec((slots, width), gate_block)] * 2 + [whole((tokens, slots))],
        out_shape=[jax.ShapeDtypeStruct((slots, hidden), F32)] * 2 + [jax.ShapeDtypeStruct((tokens, slots), BF16)],
        scratch_shapes=[pltpu.VMEM((slots, home), BF16), pltpu.VMEM((slots, rest), BF16)],
        compiler_params=pltpu.CompilerParams(vmem_limit_bytes=16 << 20),
        cost_estimate=pl.CostEstimate(
            flops=4 * slots * slots * hidden, bytes_accessed=12 * slots * hidden, transcendentals=slots * hidden
        ),
        name="factors",
    )(rank, own, spill, own, spill)


def slots_kernel(experts, rows_ref, out_ref, pick):
    @pl.when(pl.program_id(0) == 0)
    def _():
        same = slot_row(iota(pick.shape, 1), experts) == iota(pick.shape, 0)
        pick[...] = jnp.where(same, 1.0, 0.0).astype(BF16)

    out_ref[...] = plain_dot(pick[...], rows_ref[...]).astype(BF16)


def to_slot_order(rows, experts):
    slots, columns = rows.shape
    width = columns // 3
    return pl.pallas_call(
        functools.partial(slots_kernel, experts),
        grid=(3,),
        in_specs=[pl.BlockSpec((slots, width), lambda step: (0, step))],
        out_specs=pl.BlockSpec((slots, width), lambda step: (0, step)),
        out_shape=jax.ShapeDtypeStruct((slots, columns), BF16),
        scratch_shapes=[pltpu.VMEM((slots, slots), BF16)],
        compiler_params=pltpu.CompilerParams(vmem_limit_bytes=16 << 20),
        cost_estimate=pl.CostEstimate(
            flops=2 * slots * slots * columns, bytes_accessed=4 * slots * columns, transcendentals=0
        ),
        name="to_slots",
    )(rows)


def expert_kernel(experts, *refs):
    where_ref, arrived, gate_hbm, up_hbm = refs[:4]
    downs, gate_ups = refs[4 : 4 + CUTS], refs[4 + CUTS : 4 + 2 * CUTS]
    grad_ref, back_ref = refs[4 + 2 * CUTS : 6 + 2 * CUTS]
    rows, tail, pieces, down, gate_up, total, gate_factor, up_factor, grad, back_order, stage = refs[6 + 2 * CUTS : 17 + 2 * CUTS]
    row_sem, down_sem, up_sem, factor_sem, out_sem = refs[17 + 2 * CUTS :]
    full, left = experts * MAIN, experts * 2
    width = tail.shape[1]
    hidden = total.shape[1]

    def half(k):
        return pl.ds((k % 2) * width, width)

    def rows_copy(k):
        return pltpu.make_async_copy(
            arrived.at[:, columns(where_ref[k], width)], rows.at[k // 2, pl.ds(0, full), half(k)], row_sem.at[k]
        )

    def down_copy(k):
        return pltpu.make_async_copy(downs[k], down.at[k // 2, :, half(k)], down_sem.at[k])

    def gate_up_copy(k):
        return pltpu.make_async_copy(gate_ups[k], gate_up.at[k // 2, half(k)], up_sem.at[k])

    def out_copy(k, cut):
        return pltpu.make_async_copy(stage.at[k], back_ref.at[:, columns(cut, width)], out_sem.at[k])

    tail_copy = pltpu.make_async_copy(arrived.at[:, columns(CUTS, width)], tail, row_sem.at[CUTS])
    gate_copy = pltpu.make_async_copy(gate_hbm, gate_factor, factor_sem.at[0])
    up_copy = pltpu.make_async_copy(up_hbm, up_factor, factor_sem.at[1])
    tail_copy.start()
    for k in range(CUTS):
        rows_copy(k).start()
        down_copy(k).start()
    gate_copy.start()
    up_copy.start()
    order = piece_rows((full, full), 1, left)
    back_order[...] = piece_rows((full, full), 0, left)
    tail_copy.wait()
    pieces[...] = plain_dot(order, tail[...]).astype(BF16).reshape(CUTS, left, width)
    for pair in range(CUTS // 2):
        for k in (2 * pair, 2 * pair + 1):
            rows_copy(k).wait()
            down_copy(k).wait()
            rows[pair, pl.ds(full, left), half(k)] = pieces[where_ref[k]]
            if pair > 0:
                gate_up_copy(k - 2).start()
        product = rows_dot(rows[pair], down[pair])
        if pair == 0:
            total[...] = product
        elif pair < CUTS // 2 - 1:
            total[...] += product
        else:
            gate_copy.wait()
            up_copy.wait()
            for k in (2 * pair, 2 * pair + 1):
                gate_up_copy(k).start()
            hidden_cot = total[...] + product
            grad[:, :hidden] = (hidden_cot * gate_factor[...]).astype(BF16)
            grad[:, hidden:] = (hidden_cot * up_factor[...]).astype(BF16)
    grad_copy = pltpu.make_async_copy(grad, grad_ref, factor_sem.at[2])
    grad_copy.start()
    for pair in range(CUTS // 2):
        for k in (2 * pair, 2 * pair + 1):
            gate_up_copy(k).wait()
        back = rows_dot(grad[...], gate_up[pair]).astype(BF16)
        for k in (2 * pair, 2 * pair + 1):
            own = back[:, (k % 2) * width : (k % 2 + 1) * width]
            stage[k] = own[:full]
            out_copy(k, where_ref[k]).start()
            pieces[where_ref[k]] = own[full:]
    stage[CUTS] = plain_dot(back_order[...], pieces[...].reshape(full, width)).astype(BF16)
    out_copy(CUTS, CUTS).start()
    grad_copy.wait()
    for k in range(CUTS):
        out_copy(k, where_ref[k]).wait()
    out_copy(CUTS, CUTS).wait()


def expert_pass(where, arrived, gate_factor, up_factor, downs, gate_ups):
    full, length = arrived.shape
    hidden, width = downs[0].shape
    slots = gate_factor.shape[0]
    both = 2 * hidden
    model = length - width
    experts = full // MAIN
    left = experts * 2
    return pl.pallas_call(
        functools.partial(expert_kernel, experts),
        in_specs=[pl.BlockSpec(memory_space=pltpu.SMEM)] + [anywhere()] * (3 + 2 * CUTS),
        out_specs=[anywhere(), anywhere()],
        out_shape=[jax.ShapeDtypeStruct((slots, both), BF16), jax.ShapeDtypeStruct((full, length), BF16)],
        scratch_shapes=[
            pltpu.VMEM((CUTS // 2, slots, 2 * width), BF16),
            pltpu.VMEM((full, width), BF16),
            pltpu.VMEM((CUTS, left, width), BF16),
            pltpu.VMEM((CUTS // 2, hidden, 2 * width), BF16),
            pltpu.VMEM((CUTS // 2, 2 * width, both), BF16),
            pltpu.VMEM((slots, hidden), F32),
            pltpu.VMEM((slots, hidden), F32),
            pltpu.VMEM((slots, hidden), F32),
            pltpu.VMEM((slots, both), BF16),
            pltpu.VMEM((full, full), BF16),
            pltpu.VMEM((CUTS + 1, full, width), BF16),
            pltpu.SemaphoreType.DMA((CUTS + 1,)),
            pltpu.SemaphoreType.DMA((CUTS,)),
            pltpu.SemaphoreType.DMA((CUTS,)),
            pltpu.SemaphoreType.DMA((3,)),
            pltpu.SemaphoreType.DMA((CUTS + 1,)),
        ],
        compiler_params=pltpu.CompilerParams(vmem_limit_bytes=60 << 20),
        cost_estimate=pl.CostEstimate(
            flops=6 * slots * hidden * model,
            bytes_accessed=2 * (2 * slots * model + 3 * hidden * model + 2 * slots * both),
            transcendentals=0,
        ),
        name="experts",
    )(where, arrived, gate_factor, up_factor, *downs, *gate_ups)


def combine_kernel(place_ref, returned, out_ref, rows, tail, pieces, stage, row_sem, out_sem):
    full, width = tail.shape
    left = pieces.shape[1]

    def rows_copy(pair):
        return pltpu.make_async_copy(
            returned.at[:, pl.ds(pair * 2 * width, 2 * width)], rows.at[pair], row_sem.at[pair]
        )

    def out_copy(pair):
        return pltpu.make_async_copy(stage.at[pair], out_ref.at[:, pl.ds(pair * 2 * width, 2 * width)], out_sem.at[pair])

    tail_copy = pltpu.make_async_copy(returned.at[:, pl.ds(CUTS * width, width)], tail, row_sem.at[CUTS // 2])
    tail_copy.start()
    for pair in range(CUTS // 2):
        rows_copy(pair).start()
    order = piece_rows((full, full), 1, left)
    tail_copy.wait()
    pieces[...] = plain_dot(order, tail[...]).astype(BF16).reshape(CUTS, left, width)
    for pair in range(CUTS // 2):
        rows_copy(pair).wait()
        for cut in range(2):
            part = pl.ds(cut * width, width)
            total = plain_dot(place_ref[:, :full], rows[pair, :, part])
            total += plain_dot(place_ref[:, full:], pieces[2 * pair + cut])
            stage[pair, :, part] = total.astype(BF16)
        out_copy(pair).start()
    for pair in range(CUTS // 2):
        out_copy(pair).wait()


def combine(place, returned):
    full, length = returned.shape
    tokens, slots = place.shape
    width = length // (CUTS + 1)
    model = width * CUTS
    left = slots - full
    return pl.pallas_call(
        combine_kernel,
        in_specs=[in_vmem(), anywhere()],
        out_specs=anywhere(),
        out_shape=jax.ShapeDtypeStruct((tokens, model), BF16),
        scratch_shapes=[
            pltpu.VMEM((CUTS // 2, full, 2 * width), BF16),
            pltpu.VMEM((full, width), BF16),
            pltpu.VMEM((CUTS, left, width), BF16),
            pltpu.VMEM((CUTS // 2, tokens, 2 * width), BF16),
            pltpu.SemaphoreType.DMA((CUTS // 2 + 1,)),
            pltpu.SemaphoreType.DMA((CUTS // 2,)),
        ],
        compiler_params=pltpu.CompilerParams(vmem_limit_bytes=60 << 20),
        cost_estimate=pl.CostEstimate(
            flops=2 * slots * tokens * model, bytes_accessed=2 * (tokens + slots) * model, transcendentals=0
        ),
        name="combine",
    )(place, returned)


def along_dp(shard, target):
    return lax.ppermute(shard, "dp", [(i, target(i)) for i in range(lax.axis_size("dp"))])


def gathered(shard):
    count = lax.axis_size("dp")
    core = lax.axis_index("dp") & 1
    below = along_dp(shard, lambda i: (i + 2) % count)
    above = along_dp(shard, lambda i: (i - 2) % count)
    across = along_dp(jnp.where(core == 0, below, above), lambda i: (i + 2 - 4 * (i & 1)) % count)
    held = [shard, below, above, across]
    return held + [along_dp(part, lambda i: i ^ 1) for part in held]


def shard_places():
    count = lax.axis_size("dp")
    me = lax.axis_index("dp")
    steps = jnp.array([0, -2, 2, 4], jnp.int32)
    return jnp.concatenate([(me + steps + count) % count, ((me ^ 1) + steps + count) % count]).astype(jnp.int32)


def moved(rows, offset, sign):
    replicas = lax.axis_size("dp")
    for bit in range(replicas.bit_length() - 1):
        by = sign * (1 << bit)
        shifted = lax.ppermute(rows, "dp", [(i, (i + by) % replicas) for i in range(replicas)])
        rows = jnp.where(offset >> bit & 1 == 1, shifted, rows)
    return rows


def exchange(rows, experts):
    blocks = rows.reshape(experts, MAIN, rows.shape[1])
    return lax.all_to_all(blocks, "expert", split_axis=0, concat_axis=0, tiled=True).reshape(rows.shape)


def body(out_grad, route_gates, expert_ids, partner_offset, saved_pre, down_weight, gate_up_weight):
    experts = lax.axis_size("expert")
    home = experts * CAP
    offset = partner_offset[0]
    own_pre = saved_pre[0, 0]
    sent, rank = dispatch(expert_ids.T, route_gates.T, out_grad, experts)
    arrived = exchange(sent, experts)
    downs, gate_ups = gathered(down_weight[0]), gathered(gate_up_weight[0])
    spill_pre = moved(own_pre[home:], offset, -1)
    gate_factor, up_factor, place = travel_factors(rank, own_pre, spill_pre, experts)
    travel_grad, back = expert_pass(shard_places(), arrived, gate_factor, up_factor, downs, gate_ups)
    returned = exchange(back, experts)
    by_slot = to_slot_order(travel_grad, experts)
    spill_grad = moved(by_slot[home:], offset, 1)
    hidden_grad = lax.dynamic_update_slice(by_slot, spill_grad, (home, 0))
    token_grad = combine(place, returned)
    return token_grad, hidden_grad.reshape(saved_pre.shape)


def solution(mesh):
    placed = (
        P(("dp", "expert"), None),
        P(("dp", "expert"), None),
        P(("dp", "expert"), None),
        P("expert"),
        P("dp", "expert", None, None),
        P("expert", None, "dp"),
        P("expert", "dp", None),
    )
    return jax.shard_map(
        body,
        mesh=mesh,
        in_specs=placed,
        out_specs=(P(("dp", "expert"), None), P("dp", "expert", None, None)),
        check_vma=False,
    )
```

```python
import functools

import jax
import jax.numpy as jnp
from jax import lax
from jax.experimental import pallas as pl
from jax.experimental.pallas import tpu as pltpu
from jax.sharding import PartitionSpec as P

CAP = 15
OC = 3
MAIN = 16
CUTS = 8
AHEAD = 6
F32 = jnp.float32
BF16 = jnp.bfloat16


def iota(shape, axis):
    return lax.broadcasted_iota(jnp.int32, shape, axis)


def rows_dot(left, right):
    return lax.dot_general(left, right, (((1,), (1,)), ((), ())), preferred_element_type=F32)


def plain_dot(left, right):
    return lax.dot_general(left, right, (((1,), (0,)), ((), ())), preferred_element_type=F32)


def whole(shape):
    return pl.BlockSpec(shape, lambda step: (0,) * len(shape))


def piece_rows(shape, travel_axis, left):
    travelling, by_piece = iota(shape, travel_axis), iota(shape, 1 - travel_axis)
    same = travelling == ((by_piece & (left - 1)) << 3) + (by_piece >> (left.bit_length() - 1))
    return jnp.where(same, 1.0, 0.0).astype(BF16)


def anywhere():
    return pl.BlockSpec(memory_space=pl.ANY)


def in_vmem():
    return pl.BlockSpec(memory_space=pltpu.VMEM)


def columns(cut, width):
    return pl.ds(pl.multiple_of(cut * width, width), width)


def dispatch_kernel(
    experts, ids_hbm, gates_hbm, grad_ref, send_ref, rank_hbm, ids_ref, gates_ref, rank_ref, pick, scale_of, grads, stage, pieces, grad_sem, sems, small_sem
):
    choices, tokens = ids_hbm.shape
    full, left = experts * MAIN, experts * 2
    width = grads.shape[2]

    def grad_copy(cut):
        return pltpu.make_async_copy(grad_ref.at[:, pl.ds(cut * width, width)], grads.at[cut], grad_sem.at[cut])

    def send_copy(cut):
        return pltpu.make_async_copy(stage.at[cut], send_ref.at[:, pl.ds(cut * width, width)], sems.at[cut])

    ids_copy = pltpu.make_async_copy(ids_hbm, ids_ref, small_sem.at[0])
    gates_copy = pltpu.make_async_copy(gates_hbm, gates_ref, small_sem.at[1])
    rank_copy = pltpu.make_async_copy(rank_ref, rank_hbm, small_sem.at[2])
    ids_copy.start()
    gates_copy.start()
    for cut in range(CUTS):
        grad_copy(cut).start()
    earlier = (iota((tokens, tokens), 0) < iota((tokens, tokens), 1)).astype(F32).astype(BF16)
    ids_copy.wait()
    gates_copy.wait()
    expert = iota((experts, tokens), 0)
    hit = jnp.zeros((experts, tokens), F32)
    gate = jnp.zeros((experts, tokens), F32)
    for k in range(choices):
        same = ids_ref[k : k + 1, :] == expert
        hit = jnp.where(same, 1.0, hit)
        gate = jnp.where(same, gates_ref[k : k + 1, :], gate)
    rank = jnp.where(hit > 0.0, plain_dot(hit.astype(BF16), earlier), -1.0)
    rank_ref[...] = rank
    rank_copy.start()
    position = iota((experts, MAIN, tokens), 1).astype(F32)
    taken = jnp.broadcast_to(rank[:, None, :], position.shape) == position
    scale = jnp.where(taken, jnp.broadcast_to(gate[:, None, :], position.shape), 0.0)
    pick[:full] = jnp.where(taken, 1.0, 0.0).reshape(full, tokens).astype(BF16)
    scale_of[:full] = jnp.sum(scale.reshape(full, tokens), axis=1, keepdims=True)
    last = (MAIN + (iota((left, tokens), 0) & 1)).astype(F32)
    taken = rows_by(rank, left) == last
    pick[full:] = jnp.where(taken, 1.0, 0.0).astype(BF16)
    scale_of[full:] = jnp.sum(jnp.where(taken, rows_by(gate, left), 0.0), axis=1, keepdims=True)
    for cut in range(CUTS):
        grad_copy(cut).wait()
        scaled = (plain_dot(pick[...], grads[cut]) * scale_of[...]).astype(BF16)
        stage[cut] = scaled[:full]
        send_copy(cut).start()
        pieces[cut] = scaled[full:]
    stage[CUTS] = plain_dot(piece_rows((full, full), 0, left), pieces[...].reshape(full, width)).astype(BF16)
    send_copy(CUTS).start()
    for cut in range(CUTS + 1):
        send_copy(cut).wait()
    rank_copy.wait()


def rows_by(values, rows):
    n, m = values.shape
    return jnp.broadcast_to(values[:, None, :], (n, rows // n, m)).reshape(rows, m)


def dispatch(ids, gates, grad, experts):
    choices, tokens = ids.shape
    model = grad.shape[1]
    width = model // CUTS
    full, left = experts * MAIN, experts * 2
    return pl.pallas_call(
        functools.partial(dispatch_kernel, experts),
        in_specs=[anywhere()] * 3,
        out_specs=[anywhere()] * 2,
        out_shape=[
            jax.ShapeDtypeStruct((full, model + width), BF16),
            jax.ShapeDtypeStruct((experts, tokens), F32),
        ],
        scratch_shapes=[
            pltpu.VMEM((choices, tokens), jnp.int32),
            pltpu.VMEM((choices, tokens), F32),
            pltpu.VMEM((experts, tokens), F32),
            pltpu.VMEM((full + left, tokens), BF16),
            pltpu.VMEM((full + left, 1), F32),
            pltpu.VMEM((CUTS, tokens, width), BF16),
            pltpu.VMEM((CUTS + 1, full, width), BF16),
            pltpu.VMEM((CUTS, left, width), BF16),
            pltpu.SemaphoreType.DMA((CUTS,)),
            pltpu.SemaphoreType.DMA((CUTS + 1,)),
            pltpu.SemaphoreType.DMA((3,)),
        ],
        compiler_params=pltpu.CompilerParams(vmem_limit_bytes=60 << 20),
        cost_estimate=pl.CostEstimate(
            flops=2 * full * tokens * model, bytes_accessed=2 * (tokens + full) * model, transcendentals=0
        ),
        name="dispatch",
    )(ids, gates, grad)


def slot_row(index, experts):
    source, rank = index >> 4, index & (MAIN - 1)
    main = jnp.where(rank < CAP, source * CAP + rank, experts * CAP + source * OC)
    left = index - experts * MAIN
    tail = experts * CAP + (left >> 1) * OC + 1 + (left & 1)
    return jnp.where(index < experts * MAIN, main, tail)


def travel_kernel(experts, rank_ref, *refs):
    pres, (gate_ref, up_ref, place_ref, home_pick, spill_pick) = refs[:4], refs[4:]

    @pl.when(pl.program_id(0) == 0)
    def _():
        for pick, first in ((home_pick, 0), (spill_pick, experts * CAP)):
            same = slot_row(iota(pick.shape, 0), experts) == first + iota(pick.shape, 1)
            pick[...] = jnp.where(same, 1.0, 0.0).astype(BF16)
        tokens, slots = place_ref.shape
        same = jnp.where(iota((tokens, tokens), 0) == iota((tokens, tokens), 1), 1.0, 0.0).astype(BF16)
        by_token = rows_dot(same, rank_ref[...].astype(BF16)).astype(BF16)
        full = experts * MAIN

        def named(shape):
            lane = iota(shape, 1)
            left = lane - full
            of = jnp.where(lane < full, lane >> 4, left >> 1)
            at = jnp.where(lane < full, lane & (MAIN - 1), MAIN + (left & 1))
            return of, at

        of, _ = named((experts, slots))
        widen = jnp.where(of == iota((experts, slots), 0), 1.0, 0.0).astype(BF16)
        _, at = named((tokens, slots))
        place_ref[...] = jnp.where(plain_dot(by_token, widen) == at.astype(F32), 1.0, 0.0).astype(BF16)

    gate, up = (
        plain_dot(home_pick[...], own[...]) + plain_dot(spill_pick[...], spill[...])
        for own, spill in (pres[:2], pres[2:])
    )
    sigma = jax.nn.sigmoid(gate)
    gate_ref[...] = up * sigma * (1.0 + gate * (1.0 - sigma))
    up_ref[...] = gate * sigma


def travel_factors(rank, own, spill, experts):
    slots = own.shape[0]
    tokens = rank.shape[1]
    hidden = own.shape[1] // 2
    parts = 3
    width = hidden // parts
    home, rest = experts * CAP, experts * OC
    gate_block, up_block = (lambda step: (0, step)), (lambda step: (0, parts + step))
    return pl.pallas_call(
        functools.partial(travel_kernel, experts),
        grid=(parts,),
        in_specs=[
            whole((experts, tokens)),
            pl.BlockSpec((home, width), gate_block),
            pl.BlockSpec((rest, width), gate_block),
            pl.BlockSpec((home, width), up_block),
            pl.BlockSpec((rest, width), up_block),
        ],
        out_specs=[pl.BlockSpec((slots, width), gate_block)] * 2 + [whole((tokens, slots))],
        out_shape=[jax.ShapeDtypeStruct((slots, hidden), F32)] * 2 + [jax.ShapeDtypeStruct((tokens, slots), BF16)],
        scratch_shapes=[pltpu.VMEM((slots, home), BF16), pltpu.VMEM((slots, rest), BF16)],
        compiler_params=pltpu.CompilerParams(vmem_limit_bytes=16 << 20),
        cost_estimate=pl.CostEstimate(
            flops=4 * slots * slots * hidden, bytes_accessed=12 * slots * hidden, transcendentals=slots * hidden
        ),
        name="factors",
    )(rank, own, spill, own, spill)


def slots_kernel(experts, rows_ref, out_ref, pick):
    @pl.when(pl.program_id(0) == 0)
    def _():
        same = slot_row(iota(pick.shape, 1), experts) == iota(pick.shape, 0)
        pick[...] = jnp.where(same, 1.0, 0.0).astype(BF16)

    out_ref[...] = plain_dot(pick[...], rows_ref[...]).astype(BF16)


def to_slot_order(rows, experts):
    slots, columns = rows.shape
    width = columns // 3
    return pl.pallas_call(
        functools.partial(slots_kernel, experts),
        grid=(3,),
        in_specs=[pl.BlockSpec((slots, width), lambda step: (0, step))],
        out_specs=pl.BlockSpec((slots, width), lambda step: (0, step)),
        out_shape=jax.ShapeDtypeStruct((slots, columns), BF16),
        scratch_shapes=[pltpu.VMEM((slots, slots), BF16)],
        compiler_params=pltpu.CompilerParams(vmem_limit_bytes=16 << 20),
        cost_estimate=pl.CostEstimate(
            flops=2 * slots * slots * columns, bytes_accessed=4 * slots * columns, transcendentals=0
        ),
        name="to_slots",
    )(rows)


def expert_kernel(experts, *refs):
    places = shard_places()
    arrived, gate_hbm, up_hbm = refs[:3]
    downs, gate_ups = refs[3 : 3 + CUTS], refs[3 + CUTS : 3 + 2 * CUTS]
    grad_ref, back_ref = refs[3 + 2 * CUTS : 5 + 2 * CUTS]
    rows, tail, pieces, down, gate_up, total, gate_factor, up_factor, grad, back_order, stage = refs[5 + 2 * CUTS : 16 + 2 * CUTS]
    row_sem, down_sem, up_sem, factor_sem, out_sem = refs[16 + 2 * CUTS :]
    full, left = experts * MAIN, experts * 2
    width = tail.shape[1]
    hidden = total.shape[1]

    def half(k):
        return pl.ds((k % 2) * width, width)

    def rows_copy(k):
        return pltpu.make_async_copy(
            arrived.at[:, columns(places[k], width)], rows.at[k // 2, pl.ds(0, full), half(k)], row_sem.at[k]
        )

    def down_copy(k):
        return pltpu.make_async_copy(downs[k], down.at[k // 2, :, half(k)], down_sem.at[k])

    def gate_up_copy(k):
        return pltpu.make_async_copy(gate_ups[k], gate_up.at[k // 2, half(k)], up_sem.at[k])

    def out_copy(k, cut):
        return pltpu.make_async_copy(stage.at[k], back_ref.at[:, columns(cut, width)], out_sem.at[k])

    tail_copy = pltpu.make_async_copy(arrived.at[:, columns(CUTS, width)], tail, row_sem.at[CUTS])
    gate_copy = pltpu.make_async_copy(gate_hbm, gate_factor, factor_sem.at[0])
    up_copy = pltpu.make_async_copy(up_hbm, up_factor, factor_sem.at[1])
    groups = [(rows_copy(k), down_copy(k)) for k in range(CUTS)]
    groups += [(gate_copy, up_copy)] + [(gate_up_copy(k),) for k in range(CUTS)]
    groups[0] = (tail_copy,) + groups[0]

    def start(group):
        for copy in groups[group] if group < len(groups) else ():
            copy.start()

    def wait(group):
        for copy in groups[group]:
            if copy is not tail_copy:
                copy.wait()
        start(group + AHEAD)

    for group in range(AHEAD):
        start(group)
    order = piece_rows((full, full), 1, left)
    back_order[...] = piece_rows((full, full), 0, left)
    tail_copy.wait()
    pieces[...] = plain_dot(order, tail[...]).astype(BF16).reshape(CUTS, left, width)
    for pair in range(CUTS // 2):
        for k in (2 * pair, 2 * pair + 1):
            wait(k)
            rows[pair, pl.ds(full, left), half(k)] = pieces[places[k]]
            if pair == 0:
                product = rows_dot(rows[pair, :, half(k)], down[pair, :, half(k)])
                total[...] = product if k == 0 else total[...] + product
        if pair == 0:
            continue
        product = rows_dot(rows[pair], down[pair])
        if pair < CUTS // 2 - 1:
            total[...] += product
        else:
            wait(CUTS)
            hidden_cot = total[...] + product
            grad[:, :hidden] = (hidden_cot * gate_factor[...]).astype(BF16)
            grad[:, hidden:] = (hidden_cot * up_factor[...]).astype(BF16)
    grad_copy = pltpu.make_async_copy(grad, grad_ref, factor_sem.at[2])
    grad_copy.start()
    for pair in range(CUTS // 2):
        wait(CUTS + 1 + 2 * pair)
        wait(CUTS + 2 + 2 * pair)
        back = rows_dot(grad[...], gate_up[pair]).astype(BF16)
        for k in (2 * pair, 2 * pair + 1):
            own = back[:, (k % 2) * width : (k % 2 + 1) * width]
            stage[k] = own[:full]
            out_copy(k, places[k]).start()
            pieces[places[k]] = own[full:]
    stage[CUTS] = plain_dot(back_order[...], pieces[...].reshape(full, width)).astype(BF16)
    out_copy(CUTS, CUTS).start()
    grad_copy.wait()
    for k in range(CUTS):
        out_copy(k, places[k]).wait()
    out_copy(CUTS, CUTS).wait()


def expert_pass(arrived, gate_factor, up_factor, downs, gate_ups):
    full, length = arrived.shape
    hidden, width = downs[0].shape
    slots = gate_factor.shape[0]
    both = 2 * hidden
    model = length - width
    experts = full // MAIN
    left = experts * 2
    return pl.pallas_call(
        functools.partial(expert_kernel, experts),
        in_specs=[anywhere()] * (3 + 2 * CUTS),
        out_specs=[anywhere(), anywhere()],
        out_shape=[jax.ShapeDtypeStruct((slots, both), BF16), jax.ShapeDtypeStruct((full, length), BF16)],
        scratch_shapes=[
            pltpu.VMEM((CUTS // 2, slots, 2 * width), BF16),
            pltpu.VMEM((full, width), BF16),
            pltpu.VMEM((CUTS, left, width), BF16),
            pltpu.VMEM((CUTS // 2, hidden, 2 * width), BF16),
            pltpu.VMEM((CUTS // 2, 2 * width, both), BF16),
            pltpu.VMEM((slots, hidden), F32),
            pltpu.VMEM((slots, hidden), F32),
            pltpu.VMEM((slots, hidden), F32),
            pltpu.VMEM((slots, both), BF16),
            pltpu.VMEM((full, full), BF16),
            pltpu.VMEM((CUTS + 1, full, width), BF16),
            pltpu.SemaphoreType.DMA((CUTS + 1,)),
            pltpu.SemaphoreType.DMA((CUTS,)),
            pltpu.SemaphoreType.DMA((CUTS,)),
            pltpu.SemaphoreType.DMA((3,)),
            pltpu.SemaphoreType.DMA((CUTS + 1,)),
        ],
        compiler_params=pltpu.CompilerParams(vmem_limit_bytes=60 << 20),
        cost_estimate=pl.CostEstimate(
            flops=6 * slots * hidden * model,
            bytes_accessed=2 * (2 * slots * model + 3 * hidden * model + 2 * slots * both),
            transcendentals=0,
        ),
        name="experts",
    )(arrived, gate_factor, up_factor, *downs, *gate_ups)


def combine_kernel(place_hbm, returned, out_ref, place_ref, rows, tail, pieces, stage, row_sem, out_sem):
    full, width = tail.shape
    left = pieces.shape[1]

    def rows_copy(pair):
        return pltpu.make_async_copy(
            returned.at[:, pl.ds(pair * 2 * width, 2 * width)], rows.at[pair], row_sem.at[pair]
        )

    def out_copy(pair):
        return pltpu.make_async_copy(stage.at[pair], out_ref.at[:, pl.ds(pair * 2 * width, 2 * width)], out_sem.at[pair])

    tail_copy = pltpu.make_async_copy(returned.at[:, pl.ds(CUTS * width, width)], tail, row_sem.at[CUTS // 2])
    place_copy = pltpu.make_async_copy(place_hbm, place_ref, row_sem.at[CUTS // 2 + 1])
    tail_copy.start()
    place_copy.start()
    for pair in range(CUTS // 2):
        rows_copy(pair).start()
    order = piece_rows((full, full), 1, left)
    tail_copy.wait()
    pieces[...] = plain_dot(order, tail[...]).astype(BF16).reshape(CUTS, left, width)
    place_copy.wait()
    for pair in range(CUTS // 2):
        rows_copy(pair).wait()
        for cut in range(2):
            part = pl.ds(cut * width, width)
            total = plain_dot(place_ref[:, :full], rows[pair, :, part])
            total += plain_dot(place_ref[:, full:], pieces[2 * pair + cut])
            stage[pair, :, part] = total.astype(BF16)
        out_copy(pair).start()
    for pair in range(CUTS // 2):
        out_copy(pair).wait()


def combine(place, returned):
    full, length = returned.shape
    tokens, slots = place.shape
    width = length // (CUTS + 1)
    model = width * CUTS
    left = slots - full
    return pl.pallas_call(
        combine_kernel,
        in_specs=[anywhere()] * 2,
        out_specs=anywhere(),
        out_shape=jax.ShapeDtypeStruct((tokens, model), BF16),
        scratch_shapes=[
            pltpu.VMEM((tokens, slots), BF16),
            pltpu.VMEM((CUTS // 2, full, 2 * width), BF16),
            pltpu.VMEM((full, width), BF16),
            pltpu.VMEM((CUTS, left, width), BF16),
            pltpu.VMEM((CUTS // 2, tokens, 2 * width), BF16),
            pltpu.SemaphoreType.DMA((CUTS // 2 + 2,)),
            pltpu.SemaphoreType.DMA((CUTS // 2,)),
        ],
        compiler_params=pltpu.CompilerParams(vmem_limit_bytes=60 << 20),
        cost_estimate=pl.CostEstimate(
            flops=2 * slots * tokens * model, bytes_accessed=2 * (tokens + slots) * model, transcendentals=0
        ),
        name="combine",
    )(place, returned)


def along_dp(shard, target):
    return lax.ppermute(shard, "dp", [(i, target(i)) for i in range(lax.axis_size("dp"))])


def gathered(shard):
    count = lax.axis_size("dp")
    core = lax.axis_index("dp") & 1
    below = along_dp(shard, lambda i: (i + 2) % count)
    above = along_dp(shard, lambda i: (i - 2) % count)
    across = along_dp(jnp.where(core == 0, below, above), lambda i: (i + 2 - 4 * (i & 1)) % count)
    held = [shard, below, above, across]
    return held + [along_dp(part, lambda i: i ^ 1) for part in held]


def shard_places():
    count = lax.axis_size("dp")
    me = lax.axis_index("dp")
    other = me + 1 - 2 * lax.rem(me, 2)
    return [lax.rem(core + step + count, count) for core in (me, other) for step in (0, -2, 2, 4)]


def moved(rows, offset, sign):
    replicas = lax.axis_size("dp")
    for bit in range(replicas.bit_length() - 1):
        by = sign * (1 << bit)
        shifted = lax.ppermute(rows, "dp", [(i, (i + by) % replicas) for i in range(replicas)])
        rows = jnp.where(offset >> bit & 1 == 1, shifted, rows)
    return rows


def exchange(rows, experts):
    blocks = rows.reshape(experts, MAIN, rows.shape[1])
    return lax.all_to_all(blocks, "expert", split_axis=0, concat_axis=0, tiled=True).reshape(rows.shape)


def body(out_grad, route_gates, expert_ids, partner_offset, saved_pre, down_weight, gate_up_weight):
    experts = lax.axis_size("expert")
    home = experts * CAP
    offset = partner_offset[0]
    own_pre = saved_pre[0, 0]
    sent, rank = dispatch(expert_ids.T, route_gates.T, out_grad, experts)
    arrived = exchange(sent, experts)
    downs, gate_ups = gathered(down_weight[0]), gathered(gate_up_weight[0])
    spill_pre = moved(own_pre[home:], offset, -1)
    gate_factor, up_factor, place = travel_factors(rank, own_pre, spill_pre, experts)
    travel_grad, back = expert_pass(arrived, gate_factor, up_factor, downs, gate_ups)
    returned = exchange(back, experts)
    by_slot = to_slot_order(travel_grad, experts)
    spill_grad = moved(by_slot[home:], offset, 1)
    hidden_grad = lax.dynamic_update_slice(by_slot, spill_grad, (home, 0))
    token_grad = combine(place, returned)
    return token_grad, hidden_grad.reshape(saved_pre.shape)


def solution(mesh):
    placed = (
        P(("dp", "expert"), None),
        P(("dp", "expert"), None),
        P(("dp", "expert"), None),
        P("expert"),
        P("dp", "expert", None, None),
        P("expert", None, "dp"),
        P("expert", "dp", None),
    )
    return jax.shard_map(
        body,
        mesh=mesh,
        in_specs=placed,
        out_specs=(P(("dp", "expert"), None), P("dp", "expert", None, None)),
        check_vma=False,
    )
```

```python
import functools

import jax
import jax.numpy as jnp
from jax import lax
from jax.experimental import pallas as pl
from jax.experimental.pallas import tpu as pltpu
from jax.sharding import PartitionSpec as P

CAP = 15
OC = 3
MAIN = 16
CUTS = 8
AHEAD = 6
F32 = jnp.float32
BF16 = jnp.bfloat16


def iota(shape, axis):
    return lax.broadcasted_iota(jnp.int32, shape, axis)


def rows_dot(left, right):
    return lax.dot_general(left, right, (((1,), (1,)), ((), ())), preferred_element_type=F32)


def plain_dot(left, right):
    return lax.dot_general(left, right, (((1,), (0,)), ((), ())), preferred_element_type=F32)


def whole(shape):
    return pl.BlockSpec(shape, lambda step: (0,) * len(shape))


def piece_rows(shape, travel_axis, left):
    travelling, by_piece = iota(shape, travel_axis), iota(shape, 1 - travel_axis)
    same = travelling == ((by_piece & (left - 1)) << 3) + (by_piece >> (left.bit_length() - 1))
    return jnp.where(same, 1.0, 0.0).astype(BF16)


def anywhere():
    return pl.BlockSpec(memory_space=pl.ANY)


def in_vmem():
    return pl.BlockSpec(memory_space=pltpu.VMEM)


def columns(cut, width):
    return pl.ds(pl.multiple_of(cut * width, width), width)


def dispatch_kernel(
    experts, ids_hbm, gates_hbm, grad_ref, send_ref, rank_hbm, ids_ref, gates_ref, rank_ref, pick, scale_of, grads, stage, pieces, grad_sem, sems, small_sem
):
    choices, tokens = ids_hbm.shape
    full, left = experts * MAIN, experts * 2
    width = grads.shape[2] // 2

    def grad_copy(cut):
        return pltpu.make_async_copy(grad_ref.at[:, pl.ds(cut * 2 * width, 2 * width)], grads.at[cut], grad_sem.at[cut])

    def send_copy(cut):
        return pltpu.make_async_copy(stage.at[cut], send_ref.at[:, pl.ds(cut * width, width)], sems.at[cut])

    ids_copy = pltpu.make_async_copy(ids_hbm, ids_ref, small_sem.at[0])
    gates_copy = pltpu.make_async_copy(gates_hbm, gates_ref, small_sem.at[1])
    rank_copy = pltpu.make_async_copy(rank_ref, rank_hbm, small_sem.at[2])
    ids_copy.start()
    gates_copy.start()
    for pair in range(CUTS // 2):
        grad_copy(pair).start()
    earlier = (iota((tokens, tokens), 0) < iota((tokens, tokens), 1)).astype(F32).astype(BF16)
    ids_copy.wait()
    gates_copy.wait()
    expert = iota((experts, tokens), 0)
    hit = jnp.zeros((experts, tokens), F32)
    gate = jnp.zeros((experts, tokens), F32)
    for k in range(choices):
        same = ids_ref[k : k + 1, :] == expert
        hit = jnp.where(same, 1.0, hit)
        gate = jnp.where(same, gates_ref[k : k + 1, :], gate)
    rank = jnp.where(hit > 0.0, plain_dot(hit.astype(BF16), earlier), -1.0)
    rank_ref[...] = rank
    rank_copy.start()
    position = iota((experts, MAIN, tokens), 1).astype(F32)
    taken = jnp.broadcast_to(rank[:, None, :], position.shape) == position
    scale = jnp.where(taken, jnp.broadcast_to(gate[:, None, :], position.shape), 0.0)
    pick[:full] = jnp.where(taken, 1.0, 0.0).reshape(full, tokens).astype(BF16)
    scale_of[:full] = jnp.sum(scale.reshape(full, tokens), axis=1, keepdims=True)
    last = (MAIN + (iota((left, tokens), 0) & 1)).astype(F32)
    taken = rows_by(rank, left) == last
    pick[full:] = jnp.where(taken, 1.0, 0.0).astype(BF16)
    scale_of[full:] = jnp.sum(jnp.where(taken, rows_by(gate, left), 0.0), axis=1, keepdims=True)
    for pair in range(CUTS // 2):
        grad_copy(pair).wait()
        scaled = (plain_dot(pick[...], grads[pair]) * scale_of[...]).astype(BF16)
        for cut in (2 * pair, 2 * pair + 1):
            own = scaled[:, (cut % 2) * width : (cut % 2 + 1) * width]
            stage[cut] = own[:full]
            send_copy(cut).start()
            pieces[cut] = own[full:]
    stage[CUTS] = plain_dot(piece_rows((full, full), 0, left), pieces[...].reshape(full, width)).astype(BF16)
    send_copy(CUTS).start()
    for cut in range(CUTS + 1):
        send_copy(cut).wait()
    rank_copy.wait()


def rows_by(values, rows):
    n, m = values.shape
    return jnp.broadcast_to(values[:, None, :], (n, rows // n, m)).reshape(rows, m)


def dispatch(ids, gates, grad, experts):
    choices, tokens = ids.shape
    model = grad.shape[1]
    width = model // CUTS
    full, left = experts * MAIN, experts * 2
    return pl.pallas_call(
        functools.partial(dispatch_kernel, experts),
        in_specs=[anywhere()] * 3,
        out_specs=[anywhere()] * 2,
        out_shape=[
            jax.ShapeDtypeStruct((full, model + width), BF16),
            jax.ShapeDtypeStruct((experts, tokens), F32),
        ],
        scratch_shapes=[
            pltpu.VMEM((choices, tokens), jnp.int32),
            pltpu.VMEM((choices, tokens), F32),
            pltpu.VMEM((experts, tokens), F32),
            pltpu.VMEM((full + left, tokens), BF16),
            pltpu.VMEM((full + left, 1), F32),
            pltpu.VMEM((CUTS // 2, tokens, 2 * width), BF16),
            pltpu.VMEM((CUTS + 1, full, width), BF16),
            pltpu.VMEM((CUTS, left, width), BF16),
            pltpu.SemaphoreType.DMA((CUTS,)),
            pltpu.SemaphoreType.DMA((CUTS + 1,)),
            pltpu.SemaphoreType.DMA((3,)),
        ],
        compiler_params=pltpu.CompilerParams(vmem_limit_bytes=60 << 20),
        cost_estimate=pl.CostEstimate(
            flops=2 * full * tokens * model, bytes_accessed=2 * (tokens + full) * model, transcendentals=0
        ),
        name="dispatch",
    )(ids, gates, grad)


def slot_row(index, experts):
    source, rank = index >> 4, index & (MAIN - 1)
    main = jnp.where(rank < CAP, source * CAP + rank, experts * CAP + source * OC)
    left = index - experts * MAIN
    tail = experts * CAP + (left >> 1) * OC + 1 + (left & 1)
    return jnp.where(index < experts * MAIN, main, tail)


def travel_kernel(experts, rank_ref, *refs):
    pres, (gate_ref, up_ref, place_ref, home_pick, spill_pick) = refs[:4], refs[4:]

    @pl.when(pl.program_id(0) == 0)
    def _():
        for pick, first in ((home_pick, 0), (spill_pick, experts * CAP)):
            same = slot_row(iota(pick.shape, 0), experts) == first + iota(pick.shape, 1)
            pick[...] = jnp.where(same, 1.0, 0.0).astype(BF16)
        tokens, slots = place_ref.shape
        same = jnp.where(iota((tokens, tokens), 0) == iota((tokens, tokens), 1), 1.0, 0.0).astype(BF16)
        by_token = rows_dot(same, rank_ref[...].astype(BF16)).astype(BF16)
        full = experts * MAIN

        def named(shape):
            lane = iota(shape, 1)
            left = lane - full
            of = jnp.where(lane < full, lane >> 4, left >> 1)
            at = jnp.where(lane < full, lane & (MAIN - 1), MAIN + (left & 1))
            return of, at

        of, _ = named((experts, slots))
        widen = jnp.where(of == iota((experts, slots), 0), 1.0, 0.0).astype(BF16)
        _, at = named((tokens, slots))
        place_ref[...] = jnp.where(plain_dot(by_token, widen) == at.astype(F32), 1.0, 0.0).astype(BF16)

    gate, up = (
        plain_dot(home_pick[...], own[...]) + plain_dot(spill_pick[...], spill[...])
        for own, spill in (pres[:2], pres[2:])
    )
    sigma = jax.nn.sigmoid(gate)
    gate_ref[...] = up * sigma * (1.0 + gate * (1.0 - sigma))
    up_ref[...] = gate * sigma


def travel_factors(rank, own, spill, experts):
    slots = own.shape[0]
    tokens = rank.shape[1]
    hidden = own.shape[1] // 2
    parts = 3
    width = hidden // parts
    home, rest = experts * CAP, experts * OC
    gate_block, up_block = (lambda step: (0, step)), (lambda step: (0, parts + step))
    return pl.pallas_call(
        functools.partial(travel_kernel, experts),
        grid=(parts,),
        in_specs=[
            whole((experts, tokens)),
            pl.BlockSpec((home, width), gate_block),
            pl.BlockSpec((rest, width), gate_block),
            pl.BlockSpec((home, width), up_block),
            pl.BlockSpec((rest, width), up_block),
        ],
        out_specs=[pl.BlockSpec((slots, width), gate_block)] * 2 + [whole((tokens, slots))],
        out_shape=[jax.ShapeDtypeStruct((slots, hidden), F32)] * 2 + [jax.ShapeDtypeStruct((tokens, slots), BF16)],
        scratch_shapes=[pltpu.VMEM((slots, home), BF16), pltpu.VMEM((slots, rest), BF16)],
        compiler_params=pltpu.CompilerParams(vmem_limit_bytes=16 << 20),
        cost_estimate=pl.CostEstimate(
            flops=4 * slots * slots * hidden, bytes_accessed=12 * slots * hidden, transcendentals=slots * hidden
        ),
        name="factors",
    )(rank, own, spill, own, spill)


def slots_kernel(experts, rows_ref, out_ref, pick):
    @pl.when(pl.program_id(0) == 0)
    def _():
        same = slot_row(iota(pick.shape, 1), experts) == iota(pick.shape, 0)
        pick[...] = jnp.where(same, 1.0, 0.0).astype(BF16)

    out_ref[...] = plain_dot(pick[...], rows_ref[...]).astype(BF16)


def to_slot_order(rows, experts):
    slots, columns = rows.shape
    width = columns // 3
    return pl.pallas_call(
        functools.partial(slots_kernel, experts),
        grid=(3,),
        in_specs=[pl.BlockSpec((slots, width), lambda step: (0, step))],
        out_specs=pl.BlockSpec((slots, width), lambda step: (0, step)),
        out_shape=jax.ShapeDtypeStruct((slots, columns), BF16),
        scratch_shapes=[pltpu.VMEM((slots, slots), BF16)],
        compiler_params=pltpu.CompilerParams(vmem_limit_bytes=16 << 20),
        cost_estimate=pl.CostEstimate(
            flops=2 * slots * slots * columns, bytes_accessed=4 * slots * columns, transcendentals=0
        ),
        name="to_slots",
    )(rows)


def expert_kernel(experts, *refs):
    places = shard_places()
    arrived, gate_hbm, up_hbm = refs[:3]
    downs, gate_ups = refs[3 : 3 + CUTS], refs[3 + CUTS : 3 + 2 * CUTS]
    grad_ref, back_ref = refs[3 + 2 * CUTS : 5 + 2 * CUTS]
    rows, tail, pieces, down, gate_up, total, gate_factor, up_factor, grad, back_order, stage = refs[5 + 2 * CUTS : 16 + 2 * CUTS]
    row_sem, down_sem, up_sem, factor_sem, out_sem = refs[16 + 2 * CUTS :]
    full, left = experts * MAIN, experts * 2
    width = tail.shape[1]
    hidden = total.shape[1]

    def half(k):
        return pl.ds((k % 2) * width, width)

    def rows_copy(k):
        return pltpu.make_async_copy(
            arrived.at[:, columns(places[k], width)], rows.at[k // 2, pl.ds(0, full), half(k)], row_sem.at[k]
        )

    def down_copy(k):
        return pltpu.make_async_copy(downs[k], down.at[k // 2, :, half(k)], down_sem.at[k])

    def gate_up_copy(k):
        return pltpu.make_async_copy(gate_ups[k], gate_up.at[k // 2, half(k)], up_sem.at[k])

    def out_copy(k, cut):
        return pltpu.make_async_copy(stage.at[k], back_ref.at[:, columns(cut, width)], out_sem.at[k])

    tail_copy = pltpu.make_async_copy(arrived.at[:, columns(CUTS, width)], tail, row_sem.at[CUTS])
    gate_copy = pltpu.make_async_copy(gate_hbm, gate_factor, factor_sem.at[0])
    up_copy = pltpu.make_async_copy(up_hbm, up_factor, factor_sem.at[1])
    groups = [(rows_copy(k), down_copy(k)) for k in range(CUTS)]
    groups += [(gate_copy, up_copy)] + [(gate_up_copy(k),) for k in range(CUTS)]
    groups[0] = (tail_copy,) + groups[0]

    def start(group):
        for copy in groups[group] if group < len(groups) else ():
            copy.start()

    def wait(group):
        for copy in groups[group]:
            if copy is not tail_copy:
                copy.wait()
        start(group + AHEAD)

    for group in range(AHEAD):
        start(group)
    order = piece_rows((full, full), 1, left)
    back_order[...] = piece_rows((full, full), 0, left)
    tail_copy.wait()
    pieces[...] = plain_dot(order, tail[...]).astype(BF16).reshape(CUTS, left, width)
    for pair in range(CUTS // 2):
        for k in (2 * pair, 2 * pair + 1):
            wait(k)
            rows[pair, pl.ds(full, left), half(k)] = pieces[places[k]]
            if pair == 0:
                product = rows_dot(rows[pair, :, half(k)], down[pair, :, half(k)])
                total[...] = product if k == 0 else total[...] + product
        if pair == 0:
            continue
        product = rows_dot(rows[pair], down[pair])
        if pair < CUTS // 2 - 1:
            total[...] += product
        else:
            wait(CUTS)
            hidden_cot = total[...] + product
            grad[:, :hidden] = (hidden_cot * gate_factor[...]).astype(BF16)
            grad[:, hidden:] = (hidden_cot * up_factor[...]).astype(BF16)
    grad_copy = pltpu.make_async_copy(grad, grad_ref, factor_sem.at[2])
    grad_copy.start()
    for pair in range(CUTS // 2):
        wait(CUTS + 1 + 2 * pair)
        wait(CUTS + 2 + 2 * pair)
        back = rows_dot(grad[...], gate_up[pair]).astype(BF16)
        for k in (2 * pair, 2 * pair + 1):
            own = back[:, (k % 2) * width : (k % 2 + 1) * width]
            stage[k] = own[:full]
            out_copy(k, places[k]).start()
            pieces[places[k]] = own[full:]
    stage[CUTS] = plain_dot(back_order[...], pieces[...].reshape(full, width)).astype(BF16)
    out_copy(CUTS, CUTS).start()
    grad_copy.wait()
    for k in range(CUTS):
        out_copy(k, places[k]).wait()
    out_copy(CUTS, CUTS).wait()


def expert_pass(arrived, gate_factor, up_factor, downs, gate_ups):
    full, length = arrived.shape
    hidden, width = downs[0].shape
    slots = gate_factor.shape[0]
    both = 2 * hidden
    model = length - width
    experts = full // MAIN
    left = experts * 2
    return pl.pallas_call(
        functools.partial(expert_kernel, experts),
        in_specs=[anywhere()] * (3 + 2 * CUTS),
        out_specs=[anywhere(), anywhere()],
        out_shape=[jax.ShapeDtypeStruct((slots, both), BF16), jax.ShapeDtypeStruct((full, length), BF16)],
        scratch_shapes=[
            pltpu.VMEM((CUTS // 2, slots, 2 * width), BF16),
            pltpu.VMEM((full, width), BF16),
            pltpu.VMEM((CUTS, left, width), BF16),
            pltpu.VMEM((CUTS // 2, hidden, 2 * width), BF16),
            pltpu.VMEM((CUTS // 2, 2 * width, both), BF16),
            pltpu.VMEM((slots, hidden), F32),
            pltpu.VMEM((slots, hidden), F32),
            pltpu.VMEM((slots, hidden), F32),
            pltpu.VMEM((slots, both), BF16),
            pltpu.VMEM((full, full), BF16),
            pltpu.VMEM((CUTS + 1, full, width), BF16),
            pltpu.SemaphoreType.DMA((CUTS + 1,)),
            pltpu.SemaphoreType.DMA((CUTS,)),
            pltpu.SemaphoreType.DMA((CUTS,)),
            pltpu.SemaphoreType.DMA((3,)),
            pltpu.SemaphoreType.DMA((CUTS + 1,)),
        ],
        compiler_params=pltpu.CompilerParams(vmem_limit_bytes=60 << 20),
        cost_estimate=pl.CostEstimate(
            flops=6 * slots * hidden * model,
            bytes_accessed=2 * (2 * slots * model + 3 * hidden * model + 2 * slots * both),
            transcendentals=0,
        ),
        name="experts",
    )(arrived, gate_factor, up_factor, *downs, *gate_ups)


def combine_kernel(place_hbm, returned, out_ref, place_ref, rows, tail, pieces, stage, row_sem, out_sem):
    full, width = tail.shape
    left = pieces.shape[1]

    def rows_copy(pair):
        return pltpu.make_async_copy(
            returned.at[:, pl.ds(pair * 2 * width, 2 * width)], rows.at[pair], row_sem.at[pair]
        )

    def out_copy(pair):
        return pltpu.make_async_copy(stage.at[pair], out_ref.at[:, pl.ds(pair * 2 * width, 2 * width)], out_sem.at[pair])

    tail_copy = pltpu.make_async_copy(returned.at[:, pl.ds(CUTS * width, width)], tail, row_sem.at[CUTS // 2])
    place_copy = pltpu.make_async_copy(place_hbm, place_ref, row_sem.at[CUTS // 2 + 1])
    tail_copy.start()
    place_copy.start()
    for pair in range(CUTS // 2):
        rows_copy(pair).start()
    order = piece_rows((full, full), 1, left)
    tail_copy.wait()
    pieces[...] = plain_dot(order, tail[...]).astype(BF16).reshape(CUTS, left, width)
    place_copy.wait()
    for pair in range(CUTS // 2):
        rows_copy(pair).wait()
        for cut in range(2):
            part = pl.ds(cut * width, width)
            total = plain_dot(place_ref[:, :full], rows[pair, :, part])
            total += plain_dot(place_ref[:, full:], pieces[2 * pair + cut])
            stage[pair, :, part] = total.astype(BF16)
        out_copy(pair).start()
    for pair in range(CUTS // 2):
        out_copy(pair).wait()


def combine(place, returned):
    full, length = returned.shape
    tokens, slots = place.shape
    width = length // (CUTS + 1)
    model = width * CUTS
    left = slots - full
    return pl.pallas_call(
        combine_kernel,
        in_specs=[anywhere()] * 2,
        out_specs=anywhere(),
        out_shape=jax.ShapeDtypeStruct((tokens, model), BF16),
        scratch_shapes=[
            pltpu.VMEM((tokens, slots), BF16),
            pltpu.VMEM((CUTS // 2, full, 2 * width), BF16),
            pltpu.VMEM((full, width), BF16),
            pltpu.VMEM((CUTS, left, width), BF16),
            pltpu.VMEM((CUTS // 2, tokens, 2 * width), BF16),
            pltpu.SemaphoreType.DMA((CUTS // 2 + 2,)),
            pltpu.SemaphoreType.DMA((CUTS // 2,)),
        ],
        compiler_params=pltpu.CompilerParams(vmem_limit_bytes=60 << 20),
        cost_estimate=pl.CostEstimate(
            flops=2 * slots * tokens * model, bytes_accessed=2 * (tokens + slots) * model, transcendentals=0
        ),
        name="combine",
    )(place, returned)


def along_dp(shard, target):
    return lax.ppermute(shard, "dp", [(i, target(i)) for i in range(lax.axis_size("dp"))])


def gathered(shard):
    count = lax.axis_size("dp")
    core = lax.axis_index("dp") & 1
    below = along_dp(shard, lambda i: (i + 2) % count)
    above = along_dp(shard, lambda i: (i - 2) % count)
    across = along_dp(jnp.where(core == 0, below, above), lambda i: (i + 2 - 4 * (i & 1)) % count)
    held = [shard, below, above, across]
    return held + [along_dp(part, lambda i: i ^ 1) for part in held]


def shard_places():
    count = lax.axis_size("dp")
    me = lax.axis_index("dp")
    other = me + 1 - 2 * lax.rem(me, 2)
    return [lax.rem(core + step + count, count) for core in (me, other) for step in (0, -2, 2, 4)]


def moved(rows, offset, sign):
    replicas = lax.axis_size("dp")
    for bit in range(replicas.bit_length() - 1):
        by = sign * (1 << bit)
        shifted = lax.ppermute(rows, "dp", [(i, (i + by) % replicas) for i in range(replicas)])
        rows = jnp.where(offset >> bit & 1 == 1, shifted, rows)
    return rows


def exchange(rows, experts):
    blocks = rows.reshape(experts, MAIN, rows.shape[1])
    return lax.all_to_all(blocks, "expert", split_axis=0, concat_axis=0, tiled=True).reshape(rows.shape)


def body(out_grad, route_gates, expert_ids, partner_offset, saved_pre, down_weight, gate_up_weight):
    experts = lax.axis_size("expert")
    home = experts * CAP
    offset = partner_offset[0]
    own_pre = saved_pre[0, 0]
    sent, rank = dispatch(expert_ids.T, route_gates.T, out_grad, experts)
    arrived = exchange(sent, experts)
    downs, gate_ups = gathered(down_weight[0]), gathered(gate_up_weight[0])
    spill_pre = moved(own_pre[home:], offset, -1)
    gate_factor, up_factor, place = travel_factors(rank, own_pre, spill_pre, experts)
    travel_grad, back = expert_pass(arrived, gate_factor, up_factor, downs, gate_ups)
    returned = exchange(back, experts)
    by_slot = to_slot_order(travel_grad, experts)
    spill_grad = moved(by_slot[home:], offset, 1)
    hidden_grad = lax.dynamic_update_slice(by_slot, spill_grad, (home, 0))
    token_grad = combine(place, returned)
    return token_grad, hidden_grad.reshape(saved_pre.shape)


def solution(mesh):
    placed = (
        P(("dp", "expert"), None),
        P(("dp", "expert"), None),
        P(("dp", "expert"), None),
        P("expert"),
        P("dp", "expert", None, None),
        P("expert", None, "dp"),
        P("expert", "dp", None),
    )
    return jax.shard_map(
        body,
        mesh=mesh,
        in_specs=placed,
        out_specs=(P(("dp", "expert"), None), P("dp", "expert", None, None)),
        check_vma=False,
    )
```
